256 devices in a mesh: grp: 64 (over x, z, y_hi), tp: 4 (over y_lo, core).
Axes of the slice: x: 4, y: 4 (y_hi: 2, y_lo: 2; y = y_hi * 2 + y_lo), z: 8, core: 2. Of those that a mesh axis runs over, the one named last changes fastest.
Arguments:
- queries: bfloat16 [1024, 4096], P('grp', 'tp'), may hold values from -32 to 32
- prefix_kv: bfloat16 [64, 2, 1024, 2048], P('grp', None, None, 'tp'), may hold values from -12 to 12
- suffix_kv: bfloat16 [1024, 2, 32, 2048], P('grp', None, None, 'tp'), may hold values from -6 to 6
- suffix_len: int32 [1024], P('grp'), may hold values from 1 to 32, as said below
- prefill_group: int32 [64], replicated, may hold values from 0 to 63, each once
- sampler_groups: int32 [64, 4], replicated, may hold values from 0 to 63, all different within a row; in each aligned block of 64 rows (0 to 63, 64 to 127, ...) at most 8 rows name the same one
- out_weight: bfloat16 [4096, 4608], P('tp'), may hold values from -1 to 1
- norm_gain: float32 [4608], P('tp'), may hold values from 0.1 to 1.9
- residual: bfloat16 [1024, 4608], P('grp', 'tp'), may hold values from -6 to 6
Outputs:
- mixed: bfloat16 [1024, 4608], P('grp', 'tp')
The draws below stay inside these ranges and needn't reach their ends.
Inputs may be any that keep to these rules, and one draw needn't show every extreme that they name: `suffix_len`: some sample has all 32 slots live. `prefill_group`: each group prefilled exactly one prompt. `sampler_groups`: a row names 4 different groups; every group is named by 1 to 8 rows, a bound that some block reaches.
All inputs are finite; a program needn't handle non-finite values.
Results may differ from the reference program's by a relative error of at most 0.015.
Values may be sent and summed in bfloat16 or wider, within the bound.
A program may use at most 128 MiB of HBM per device.

```python
import math
import jax
import jax.numpy as jnp
import numpy as np
from jax import lax

D = 4608
QH = 32
KVH = 16
HD = 128
PREFIX = 1024
SUF = 32
SAMP = 16
SAMPLERS = 4
MOSTP = 8
PROMPTS = 64
SAMPLES = 1024
N_GRP = 64


def draw_queries(key, part):
    key = jax.random.fold_in(key, 11)
    base = jnp.clip(jax.random.normal(key, (SAMPLES, QH, HD), jnp.float32), -6.0, 6.0)
    return base.reshape(SAMPLES, QH * HD).astype(jnp.bfloat16)


def draw_prefix_kv(key, part):
    key = jax.random.fold_in(key, 12)
    shape = (PROMPTS, 2, PREFIX, KVH, HD)
    base = jnp.clip(jax.random.normal(key, shape, jnp.float32), -6.0, 6.0)
    return base.reshape(PROMPTS, 2, PREFIX, KVH * HD).astype(jnp.bfloat16)


def draw_suffix_len(key, part):
    key = jax.random.fold_in(key, 13)
    first, second, third = jax.random.split(key, 3)
    lengths = jax.random.randint(first, (SAMPLES,), 1, SUF + 1)
    index = jnp.arange(SAMPLES, dtype=jnp.int32)
    longest = jax.random.randint(second, (), 0, SAMPLES)
    shortest = (longest + 1 + jax.random.randint(third, (), 0, SAMPLES - 1)) % SAMPLES
    lengths = jnp.where(index == longest, SUF, lengths)
    lengths = jnp.where(index == shortest, 1, lengths)
    return lengths.astype(jnp.int32)


def draw_out_weight(key, part):
    key = jax.random.fold_in(key, 14)
    first, second = jax.random.split(key)
    base = jnp.clip(jax.random.normal(first, (QH * HD, D), jnp.float32), -4.0, 4.0)
    column = jnp.arange(D, dtype=jnp.float32) / D
    column_scale = jnp.exp(jnp.log(3.0) * column + jax.random.uniform(second, (D,), jnp.float32, -1.15, 1.15))
    scaled = base * column_scale[None, :] * (QH * HD) ** (-0.5)
    return jnp.clip(scaled, -1.0, 1.0).astype(jnp.bfloat16)


def block_levels(stream_key, dims, shards, least, top_value):
    def one(dim, parts):
        steps = jax.random.uniform(jax.random.fold_in(jax.random.fold_in(stream_key, 6), dim), (parts,), jnp.float32, least / len(shards), top_value / len(shards))
        return jnp.repeat(jnp.exp(steps), dims[dim] // parts).reshape((-1,) + (1,) * (len(dims) - dim - 1))

    loudness = one(*shards[0])
    for cut in shards[1:]:
        loudness = loudness * one(*cut)
    return loudness


def shared_out(key, own, number, rows, number_of, top, limit, lean):
    order = jax.random.permutation(key, number_of)
    packed, ordinary = shares(number_of, rows * top, limit, lean, True), shares(number_of, rows * top, limit, lean, False)
    places = jnp.arange(number_of)

    def named(sizes, rotation):
        used = int((sizes > 0).sum())
        fixed = max(1, used // 4)
        passed = fixed + (places - fixed + rotation * (used - fixed)) % max(1, number_of - fixed)
        return jnp.zeros((number_of,), jnp.int32).at[order[jnp.where(places < fixed, places, passed)]].set(jnp.asarray(sizes, jnp.int32))

    sizes = jnp.where(number % 4 == 0, named(packed, number // 4), named(ordinary, number - number // 4 - 1))
    mixed = jax.random.permutation(jax.random.fold_in(own, 3), number_of)
    giver, taker = mixed[0:number_of // 2 * 2:2], mixed[1:number_of // 2 * 2:2]
    margin = jnp.minimum(sizes[giver] - 1, limit - sizes[taker]) // 2
    margin = jnp.where((giver == order[0]) | (taker == order[0]) | (sizes[taker] == 0), 0, jnp.maximum(margin, 0))
    passed = jax.random.randint(jax.random.fold_in(own, 4), (number_of // 2,), 0, 1 << 20) % (margin + 1)
    sizes = sizes.at[giver].add(-passed).at[taker].add(passed)
    items = jnp.searchsorted(jnp.cumsum(sizes), jnp.arange(rows * top), side="right").astype(jnp.int32)
    table = items.reshape(top, rows).T
    table = table[jax.random.permutation(jax.random.fold_in(own, 1), rows)]
    rotation = jax.random.randint(jax.random.fold_in(own, 2), (rows, 1), 0, top)
    return jnp.take_along_axis(table, (jnp.arange(top)[None, :] + rotation) % top, axis=1)


def shares(count, total, limit, skew, full):
    portions = [(1 << 20) // math.isqrt(rank ** skew) + 1 for rank in range(1, count + 1)]
    largest = limit if full else min(limit, max(-(-total // count), total * portions[0] // sum(portions)))
    least = 1 if total - largest >= count - 1 else 0
    counts, rest = [largest] + [least] * (count - 1), total - largest - least * (count - 1)
    while rest > 0:
        free = [i for i in range(1, count) if counts[i] < largest] or [i for i in range(1, count) if counts[i] < limit]
        pool, budget = sum([portions[i] for i in free]), rest
        for i in free:
            more = min(limit - counts[i], max(1, budget * portions[i] // pool), rest)
            counts[i] = counts[i] + more
            rest = rest - more
    return np.array(counts)


def centred(own_key, extent, scale, most, shards=(), held_as=jnp.bfloat16):
    drawn = jax.random.normal(own_key, extent, jnp.float32) * scale
    if len(shards) > 0:
        drawn = block_levels(own_key, extent, shards, -0.22, 0.18) * drawn
    return jnp.clip(drawn, min=-most, max=most).astype(held_as)


def setup_inputs(seed: int = 0) -> dict:
    streams_of = jax.random.split(jax.random.key(seed), 10)
    queries = draw_queries(jax.random.fold_in(streams_of[9], 71), 0)
    prefix_kv = draw_prefix_kv(jax.random.fold_in(streams_of[9], 71), 0)
    suffix_kv = centred(streams_of[2], (SAMPLES, 2, SUF, KVH * HD), 1.0, 6.0, ((0, 64), (3, 4)))
    suffix_len = draw_suffix_len(jax.random.fold_in(streams_of[9], 71), 0)
    prefill_group = jax.random.permutation(streams_of[4], N_GRP).astype(jnp.int32)
    sampler_groups_keys = jax.random.split(jax.random.fold_in(streams_of[5], 1), PROMPTS // PROMPTS)
    sampler_groups_turns = jax.random.permutation(jax.random.fold_in(streams_of[5], 3), PROMPTS // PROMPTS)
    sampler_groups = jax.vmap(lambda own, number: shared_out(jax.random.fold_in(streams_of[5], 2), own, number, PROMPTS, N_GRP, SAMPLERS, MOSTP, 2))(sampler_groups_keys, sampler_groups_turns).reshape((PROMPTS, SAMPLERS))
    out_weight = draw_out_weight(jax.random.fold_in(streams_of[9], 71), 0)
    norm_gain = jnp.clip(1.0 + 0.18 * jax.random.normal(streams_of[7], (D,), jnp.float32), 0.1, 1.9)
    residual = centred(streams_of[8], (SAMPLES, D), 1.0, 6.0, ((0, 64), (1, 4)))
    return dict(queries=queries, prefix_kv=prefix_kv, suffix_kv=suffix_kv, suffix_len=suffix_len, prefill_group=prefill_group, sampler_groups=sampler_groups, out_weight=out_weight, norm_gain=norm_gain, residual=residual)


score_scale = 144.0 ** (-0.5)
norm_eps = 1e-06

def sample_owners(prefill_group, sampler_groups, per_group):
    prompt_total = prefill_group.shape[0]
    group_ids = jnp.arange(prompt_total, dtype=jnp.int32)
    member = jnp.any(sampler_groups[None, :, :] == group_ids[:, None, None], axis=2).astype(jnp.int32)
    slot_rank = jnp.cumsum(member, axis=1) - member
    prompt_count = jnp.maximum(lax.optimization_barrier(jnp.sum(member, axis=1)), 1)
    slot_ids = jnp.arange(per_group, dtype=jnp.int32)
    wanted = slot_ids[None, :] % prompt_count[:, None]
    chosen = ((member[:, None, :] == 1) & (slot_rank[:, None, :] == wanted[:, :, None])).astype(jnp.int32)
    return lax.optimization_barrier(jnp.sum(chosen * prefill_group[None, None, :], axis=2)).astype(jnp.int32)

def prefix_partial(query_rows, prefix_keys, prefix_values):
    row_count = query_rows.shape[0]
    key_count = prefix_keys.shape[0]
    kv_count = prefix_keys.shape[1] // HD
    group_size = query_rows.shape[1] // prefix_keys.shape[1]
    query_heads = jnp.transpose(query_rows.reshape(row_count, kv_count, group_size, HD), (1, 0, 2, 3))
    key_heads = jnp.transpose(prefix_keys.reshape(key_count, kv_count, HD), (1, 0, 2))
    value_heads = jnp.transpose(prefix_values.reshape(key_count, kv_count, HD), (1, 0, 2))

    def one_head(pieces):
        query_one, key_one, value_one = pieces
        scores = jnp.einsum('rgd,td->rgt', query_one.astype(jnp.float32), key_one.astype(jnp.float32)) * score_scale
        row_max = lax.optimization_barrier(jnp.max(scores, axis=2))
        weights = jnp.exp(scores - row_max[..., None])
        denominator = lax.optimization_barrier(jnp.sum(weights, axis=2))
        rounded = weights.astype(jnp.bfloat16).astype(jnp.float32)
        weighted = jnp.einsum('rgt,td->rgd', rounded, value_one.astype(jnp.float32))
        return ((weighted / denominator[..., None]).astype(jnp.bfloat16), row_max + jnp.log(denominator))
    outs, log_total = lax.map(one_head, (query_heads, key_heads, value_heads))
    outs = jnp.transpose(outs, (1, 0, 2, 3)).reshape(row_count, kv_count * group_size * HD)
    log_total = jnp.transpose(log_total, (1, 0, 2)).reshape(row_count, kv_count * group_size)
    return (outs, log_total)

def suffix_partial(query_rows, suffix_kv, suffix_len):
    row_count = suffix_kv.shape[0]
    length = suffix_kv.shape[2]
    kv_count = suffix_kv.shape[3] // HD
    group_size = query_rows.shape[1] // suffix_kv.shape[3]
    query_heads = query_rows.reshape(row_count, kv_count, group_size, HD).astype(jnp.float32)
    key_heads = suffix_kv[:, 0].reshape(row_count, length, kv_count, HD).astype(jnp.float32)
    value_heads = suffix_kv[:, 1].reshape(row_count, length, kv_count, HD).astype(jnp.float32)
    scores = jnp.einsum('skgd,stkd->skgt', query_heads, key_heads) * score_scale
    is_live = (jnp.arange(length, dtype=jnp.int32)[None, :] < suffix_len[:, None])[:, None, None, :]
    row_max = lax.optimization_barrier(jnp.max(jnp.where(is_live, scores, -jnp.inf), axis=3))
    weights = jnp.where(is_live, jnp.exp(scores - row_max[..., None]), 0.0)
    denominator = lax.optimization_barrier(jnp.sum(weights, axis=3))
    rounded = weights.astype(jnp.bfloat16).astype(jnp.float32)
    weighted = jnp.einsum('skgt,stkd->skgd', rounded, value_heads)
    outs = (weighted / denominator[..., None]).reshape(row_count, kv_count * group_size, HD)
    return (outs, (row_max + jnp.log(denominator)).reshape(row_count, kv_count * group_size))

def combine_parts(prefix_out, prefix_log, suffix_out, suffix_log):
    row_count = prefix_out.shape[0]
    heads = prefix_log.shape[1]
    joint_max = jnp.maximum(prefix_log, suffix_log)
    prefix_share = jnp.exp(prefix_log - joint_max)
    suffix_share = jnp.exp(suffix_log - joint_max)
    merged = (prefix_share[..., None] * prefix_out.reshape(row_count, heads, HD).astype(jnp.float32) + suffix_share[..., None] * suffix_out) / (prefix_share + suffix_share)[..., None]
    return merged.reshape(row_count, heads * HD).astype(jnp.bfloat16)

def reference(queries, prefix_kv, suffix_kv, suffix_len, prefill_group, sampler_groups, out_weight, norm_gain, residual):
    owners = sample_owners(prefill_group, sampler_groups, SAMP).reshape(-1)

    def per_sample(inputs):
        query_row, owner = inputs
        sample_kv = lax.dynamic_index_in_dim(prefix_kv, owner, 0, keepdims=False)
        outs, log_total = prefix_partial(query_row[None], sample_kv[0], sample_kv[1])
        return (outs[0], log_total[0])
    prefix_out, prefix_log = lax.map(per_sample, (queries, owners))
    suffix_out, suffix_log = suffix_partial(queries, suffix_kv, suffix_len)
    attended = combine_parts(prefix_out, prefix_log, suffix_out, suffix_log)
    projected = jnp.dot(attended, out_weight, preferred_element_type=jnp.float32)
    scale = lax.rsqrt(lax.optimization_barrier(jnp.mean(projected * projected, axis=1, keepdims=True)) + norm_eps)
    return (residual.astype(jnp.float32) + projected * scale * norm_gain[None, :]).astype(jnp.bfloat16)
```

```python
import jax
import jax.numpy as jnp
from jax import lax
from jax.experimental import pallas as pl
from jax.experimental.pallas import tpu as pltpu
from jax.sharding import PartitionSpec as P

MESH = pl.DeviceIdType.MESH
D = 4608
HD = 128
SAMP = 16
SLOTS = 4
PREFIX = 1024
SUF = 32
HEADS = 8
KVHEADS = 4
COLS = 1152
PROMPTS = 64
SCORE_SCALE = 144.0 ** (-0.5)
NORM_EPS = 1e-06
NEG = -1e30

Z_FAR = (4, 3, 5, 2, 6, 1, 7)
Z_NEAR = (1, 7, 2, 6, 3, 5, 4)
B_FAR = ((2, 1), (1, 1), (3, 1), (2, 0), (0, 1), (1, 0), (3, 0))

f32 = jnp.float32
bf16 = jnp.bfloat16
i32 = jnp.int32


def kernel(
    q_hbm, kv_hbm, suf_hbm, len_hbm, pre_hbm, sam_hbm, w_hbm, gain_hbm, res_hbm,
    o_ref,
    qh, kv, suf, w, gain, res, len_s, pre_s, sam_s, sam_v,
    own_p, pick_s,
    qall, csend, qc, rsend, rc, bsend, bt, asend, fin,
    hot, hot2, lmask, suf_o, suf_l, psend, pr, sqs, sqr,
    lq, lkv, lsuf, lw, lsmall, lint,
    sa, ra, sb, rb, sc, rcs, sct, rct, sbt, rbt, sat, rat, srs, rrs, ssq, rsq,
):
    me = lax.axis_index("grp")
    tp = lax.axis_index("tp")
    x = me // 16
    z = (me // 2) % 8
    yh = me % 2
    b = x * 2 + yh

    def grp_of(xx, zz, yy):
        return (xx * 8 + zz) * 2 + yy

    def z_peer(off):
        zz = (z + off) % 8
        return zz, (grp_of(x, zz, yh), tp)

    def b_peer(off):
        xx = (x + off[0]) % 4
        yy = (yh + off[1]) % 2
        return xx * 2 + yy, (grp_of(xx, z, yy), tp)

    def tp_peer(off):
        yy, cc = (tp // 2 + off // 2) % 2, (tp % 2 + off % 2) % 2
        return yy * 2 + cc, (me, yy * 2 + cc)

    def remote(src, dst, send, recv, device):
        return pltpu.make_async_remote_copy(
            src_ref=src, dst_ref=dst, send_sem=send, recv_sem=recv,
            device_id=device, device_id_type=MESH,
        )

    barrier = pltpu.get_barrier_semaphore()
    for off in Z_FAR:
        pl.semaphore_signal(barrier, inc=1, device_id=z_peer(off)[1], device_id_type=MESH)
    for off in B_FAR:
        pl.semaphore_signal(barrier, inc=1, device_id=b_peer(off)[1], device_id_type=MESH)
    for off in (2, 3, 1):
        pl.semaphore_signal(barrier, inc=1, device_id=tp_peer(off)[1], device_id_type=MESH)

    ints = [
        pltpu.make_async_copy(pre_hbm, pre_s, lint.at[0]),
        pltpu.make_async_copy(sam_hbm, sam_s, lint.at[1]),
        pltpu.make_async_copy(sam_hbm, sam_v, lint.at[2]),
        pltpu.make_async_copy(len_hbm, len_s, lint.at[3]),
    ]
    for copy in ints:
        copy.start()
    for i in range(HEADS):
        pltpu.make_async_copy(q_hbm.at[:, pl.ds(i * HD, HD)], qh.at[i], lq).start()
    for part in range(2):
        for k in range(KVHEADS):
            pltpu.make_async_copy(
                kv_hbm.at[0, part, :, pl.ds(k * HD, HD)], kv.at[part, k], lkv
            ).start()
    for part in range(2):
        for k in range(KVHEADS):
            pltpu.make_async_copy(
                suf_hbm.at[:, part, :, pl.ds(k * HD, HD)], suf.at[part, k], lsuf
            ).start()
    small = [
        pltpu.make_async_copy(gain_hbm, gain, lsmall.at[0]),
        pltpu.make_async_copy(res_hbm, res, lsmall.at[1]),
    ]
    for copy in small:
        copy.start()
    for t in range(4):
        pltpu.make_async_copy(w_hbm.at[:, pl.ds(t * COLS, COLS)], w.at[t], lw).start()

    for copy in ints:
        copy.wait()

    line = [z_peer(off)[1][0] for off in range(8)]

    def find(p, found):
        group = pre_s[p]
        return tuple(found[off] + jnp.where(group == line[off], p, 0) for off in range(8))

    found = lax.fori_loop(0, PROMPTS, find, (jnp.int32(0),) * 8)
    for off in range(8):
        own_p[off] = found[off]
        for s in range(SLOTS):
            pick_s[off * SLOTS + s] = sam_s[s, found[off] & 63]

    pltpu.make_async_copy(qh, qh, lq).wait()
    pl.semaphore_wait(barrier, 17)

    for off in Z_FAR:
        zz, device = z_peer(off)
        remote(qh.at[zz], qall.at[off], sa, ra.at[off], device).start()
    qall[0] = qh[z]

    for off in (0,) + Z_NEAR:
        block = qall.at[off]
        if off != 0:
            remote(qh.at[0], block, sa, ra.at[off], (me, tp)).wait_recv()
        for boff in B_FAR:
            slot = (boff[0] * 2 + boff[1]) * 8 + off
            remote(block, qall.at[slot], sb, rb, b_peer(boff)[1]).start()
    others = qall.at[pl.ds(8, 56)]
    remote(others, others, sb, rb, (me, tp)).wait_recv()

    for off in Z_FAR + (0,):
        for s in range(SLOTS):
            g = pick_s[off * SLOTS + s]
            slot = (((x - (g >> 4)) & 3) * 2 + ((yh - g) & 1)) * 8 + ((z - (g >> 1)) & 7)
            block = qall[slot]
            if off == 0:
                qc[0, pl.ds(s * SAMP, SAMP)] = block
            else:
                csend[off, pl.ds(s * SAMP, SAMP)] = block
        if off != 0:
            remote(csend.at[off], qc.at[off], sc, rcs.at[off], z_peer(off)[1]).start()

    lane = lax.broadcasted_iota(i32, (1, 512), 1)
    lane_block = lane >> 4
    lane_row = lane & 15
    group_lane = jnp.zeros((1, 512), i32)
    prompt_lane = jnp.zeros((1, 512), i32)
    for c in range(32):
        group_lane = jnp.where(lane_block == c, pick_s[c], group_lane)
    for off in range(8):
        prompt_lane = jnp.where((lane >> 6) == off, own_p[off], prompt_lane)
    pick_b = (((group_lane >> 4) - x) & 3) * 2 + ((group_lane - yh) & 1)
    pick_z = ((group_lane >> 1) - z) & 7
    table = jnp.transpose(sam_v[...])
    member = jnp.zeros((PROMPTS, 512), f32)
    for s in range(SLOTS):
        member = member + jnp.where(table[:, s : s + 1] == group_lane, 1.0, 0.0)
    prompt_row = lax.broadcasted_iota(i32, (PROMPTS, 512), 0)
    count = jnp.sum(member, axis=0, keepdims=True)
    rank = jnp.sum(jnp.where(prompt_row < prompt_lane, member, 0.0), axis=0, keepdims=True)
    row = lane_row.astype(f32)
    rest = row - jnp.floor((row + 0.5) / count) * count
    owned = rest == rank
    place = jnp.where(owned, (pick_b * 8 + pick_z) * SAMP + lane_row, -1)
    place2 = jnp.where(owned, pick_b * SAMP + lane_row, -1)
    rows = lax.broadcasted_iota(i32, (128, 512), 0)
    for bb in range(8):
        hot[bb] = jnp.where(rows + bb * 128 == place, 1.0, 0.0).astype(bf16)
    hot2[...] = jnp.where(rows == place2, 1.0, 0.0).astype(bf16)
    tile_lane = lax.broadcasted_iota(i32, (SAMP, HD), 1)
    for c in range(32):
        of_z = ((pick_s[c] >> 1) - z) & 7
        keep = ((tile_lane >> 3) == of_z) & (((tile_lane & 7) >> 1) == c % SLOTS)
        lmask[pl.ds(c * SAMP, SAMP)] = jnp.where(keep, 1.0, 0.0).astype(bf16)

    pltpu.make_async_copy(kv, kv, lkv).wait()
    for off in (0,) + Z_NEAR:
        if off != 0:
            remote(csend.at[off], qc.at[off], sc, rcs.at[off], (me, tp)).wait_recv()
        head, device = z_peer(-off)
        k = head // 2
        scores = (
            lax.dot_general(
                qc[off], kv[0, k], (((1,), (1,)), ((), ())), preferred_element_type=f32
            )
            * SCORE_SCALE
        )
        top = jnp.max(scores, axis=1, keepdims=True)
        weights = jnp.exp(scores - top)
        total = jnp.sum(weights, axis=1, keepdims=True)
        out = jnp.dot(weights.astype(bf16), kv[1, k], preferred_element_type=f32) / total
        log_total = top + jnp.log(total)
        high = log_total.astype(bf16).astype(f32)
        low = log_total - high
        tile = jnp.zeros((SAMP, HD), f32)
        for s in range(SLOTS):
            at = s * SAMP
            tile = jnp.where((tile_lane & 7) == 2 * s, high[at : at + SAMP], tile)
            tile = jnp.where((tile_lane & 7) == 2 * s + 1, low[at : at + SAMP], tile)
        result = rc if off == 0 else rsend
        result[off, pl.ds(0, 64)] = out.astype(bf16)
        result[off, pl.ds(64, SAMP)] = tile.astype(bf16)
        if off != 0:
            remote(rsend.at[off], rc.at[off], sct, rct, device).start()

    pltpu.make_async_copy(suf, suf, lsuf).wait()
    col = lax.broadcasted_iota(i32, (32, 512), 1)
    srow = lax.broadcasted_iota(i32, (32, 512), 0) & 15
    col_sample = col >> 5
    live_len = jnp.zeros((32, 512), i32)
    for s in range(SAMP):
        live_len = jnp.where(col_sample == s, len_s[s], live_len)
    live = (col_sample == srow) & ((col & 31) < live_len)
    for k in range(KVHEADS):
        query = qh[pl.ds(2 * k, 2)].reshape(32, HD)
        scores = (
            lax.dot_general(
                query, suf[0, k].reshape(512, HD), (((1,), (1,)), ((), ())),
                preferred_element_type=f32,
            )
            * SCORE_SCALE
        )
        top = jnp.max(jnp.where(live, scores, NEG), axis=1, keepdims=True)
        weights = jnp.where(live, jnp.exp(jnp.where(live, scores - top, 0.0)), 0.0)
        total = jnp.sum(weights, axis=1, keepdims=True)
        out = (
            jnp.dot(weights.astype(bf16), suf[1, k].reshape(512, HD), preferred_element_type=f32)
            / total
        )
        suf_o[pl.ds(k * 32, 32)] = out
        suf_l[pl.ds(k * 32, 32)] = jnp.broadcast_to(top + jnp.log(total), (32, HD))

    seven = rc.at[pl.ds(1, 7)]
    remote(seven, seven, sct, rct, (me, tp)).wait_recv()
    results = rc[:, pl.ds(0, 64)].reshape(512, HD)
    logs = jnp.concatenate(
        [rc[off, pl.ds(64, SAMP)] for off in range(8) for _ in range(SLOTS)], axis=0
    ) * lmask[...]
    log_rows = jnp.dot(hot2[...], logs, preferred_element_type=f32).astype(bf16)

    for boff in B_FAR + ((0, 0),):
        n = boff[0] * 2 + boff[1]
        picked = jnp.dot(hot[n], results, preferred_element_type=f32).astype(bf16)
        block = bt if n == 0 else bsend
        block[n, pl.ds(0, 128)] = picked
        block[n, pl.ds(128, SAMP)] = log_rows[n * SAMP : (n + 1) * SAMP]
        if n != 0:
            remote(bsend.at[n], bt.at[n], sbt, rbt, b_peer(boff)[1]).start()
    seven = bt.at[pl.ds(1, 7)]
    remote(seven, seven, sbt, rbt, (me, tp)).wait_recv()

    merged = bt[0].astype(f32)
    for n in range(1, 8):
        merged = merged + bt[n].astype(f32)
    merged = merged.astype(bf16)
    for off in Z_FAR + (0,):
        block = fin if off == 0 else asend
        block[off, pl.ds(0, SAMP)] = merged[off * SAMP : (off + 1) * SAMP]
        block[off, pl.ds(SAMP, SAMP)] = merged[128:144]
        if off != 0:
            remote(asend.at[off], fin.at[off], sat, rat, z_peer(off)[1]).start()
    pltpu.make_async_copy(w, w, lw).wait()
    seven = fin.at[pl.ds(1, 7)]
    remote(seven, seven, sat, rat, (me, tp)).wait_recv()

    come = [fin[(z - i) % 8] for i in range(HEADS)]
    prefix_out = jnp.concatenate([block[:SAMP] for block in come], axis=0).astype(f32)
    log_tile = jnp.concatenate([block[SAMP:] for block in come], axis=0).astype(f32)
    all_lane = lax.broadcasted_iota(i32, (128, HD), 1)
    all_row = lax.broadcasted_iota(i32, (128, HD), 0)
    prefix_log = jnp.sum(
        jnp.where((all_lane >> 3) == ((z - (all_row >> 4)) & 7), log_tile, 0.0),
        axis=1, keepdims=True,
    )
    suffix_log = suf_l[...]
    joint = jnp.maximum(prefix_log, suffix_log)
    share_p = jnp.exp(prefix_log - joint)
    share_s = jnp.exp(suffix_log - joint)
    attended = (
        (share_p * prefix_out + share_s * suf_o[...]) / (share_p + share_s)
    ).astype(bf16)
    attended = jnp.concatenate(
        [attended[i * SAMP : (i + 1) * SAMP] for i in range(HEADS)], axis=1
    )

    for off in (2, 3, 1):
        tt, device = tp_peer(off)
        psend[off - 1] = jnp.dot(attended, w[tt], preferred_element_type=f32).astype(bf16)
        remote(psend.at[off - 1], pr.at[off - 1], srs, rrs, device).start()
    projected = jnp.dot(attended, w[tp], preferred_element_type=f32)
    remote(psend, pr, srs, rrs, (me, tp)).wait_recv()
    for off in range(3):
        projected = projected + pr[off].astype(f32)
    squares = jnp.zeros((SAMP, HD), f32)
    for n in range(COLS // HD):
        piece = projected[:, n * HD : (n + 1) * HD]
        squares = squares + piece * piece
    sqs[...] = squares
    for off in (2, 3, 1):
        remote(sqs, sqr.at[off - 1], ssq.at[off - 1], rsq, tp_peer(off)[1]).start()
    for copy in small:
        copy.wait()
    remote(sqr, sqr, ssq.at[0], rsq, (me, tp)).wait_recv()
    for off in range(3):
        squares = squares + sqr[off]
    scale = lax.rsqrt(jnp.sum(squares, axis=1, keepdims=True) / D + NORM_EPS)
    o_ref[...] = (res[...].astype(f32) + projected * scale * gain[...].reshape(1, COLS)).astype(bf16)

    seven = qall.at[pl.ds(0, 7)]
    remote(seven, seven, sa, ra.at[0], (me, tp)).wait_send()
    seven = qall.at[pl.ds(0, 56)]
    remote(seven, seven, sb, rb, (me, tp)).wait_send()
    for ref, send, recv in (
        (csend, sc, rcs.at[0]), (rc, sct, rct), (bt, sbt, rbt), (fin, sat, rat)
    ):
        seven = ref.at[pl.ds(0, 7)]
        remote(seven, seven, send, recv, (me, tp)).wait_send()
    remote(psend, pr, srs, rrs, (me, tp)).wait_send()
    for off in range(3):
        remote(sqs, sqr.at[off], ssq.at[off], rsq, (me, tp)).wait_send()


def shards(
    queries, prefix_kv, suffix_kv, suffix_len, prefill_group, sampler_groups,
    out_weight, norm_gain, residual,
):
    vmem = pltpu.VMEM
    dma = pltpu.SemaphoreType.DMA
    scratch = [
        vmem((HEADS, SAMP, HD), bf16),
        vmem((2, KVHEADS, PREFIX, HD), bf16),
        vmem((2, KVHEADS, SAMP, SUF, HD), bf16),
        vmem((4, HEADS * HD, COLS), bf16),
        vmem((COLS,), f32),
        vmem((SAMP, COLS), bf16),
        pltpu.SMEM((SAMP,), i32),
        pltpu.SMEM((PROMPTS,), i32),
        pltpu.SMEM((SLOTS, PROMPTS), i32),
        vmem((SLOTS, PROMPTS), i32),
        pltpu.SMEM((8,), i32),
        pltpu.SMEM((32,), i32),
        vmem((64, SAMP, HD), bf16),
        vmem((8, 64, HD), bf16),
        vmem((8, 64, HD), bf16),
        vmem((8, 80, HD), bf16),
        vmem((8, 80, HD), bf16),
        vmem((8, 144, HD), bf16),
        vmem((8, 144, HD), bf16),
        vmem((8, 32, HD), bf16),
        vmem((8, 32, HD), bf16),
        vmem((8, 128, 512), bf16),
        vmem((128, 512), bf16),
        vmem((512, HD), bf16),
        vmem((128, HD), f32),
        vmem((128, HD), f32),
        vmem((3, SAMP, COLS), bf16),
        vmem((3, SAMP, COLS), bf16),
        vmem((SAMP, HD), f32),
        vmem((3, SAMP, HD), f32),
        dma, dma, dma, dma, dma((2,)), dma((4,)),
        dma, dma((8,)),
        dma, dma,
        dma, dma((8,)),
        dma, dma,
        dma, dma,
        dma, dma,
        dma, dma,
        dma((3,)), dma,
    ]
    anywhere = pl.BlockSpec(memory_space=pl.ANY)
    return pl.pallas_call(
        kernel,
        out_shape=jax.ShapeDtypeStruct(residual.shape, bf16),
        in_specs=[anywhere] * 9,
        out_specs=pl.BlockSpec(memory_space=pltpu.VMEM),
        scratch_shapes=scratch,
        compiler_params=pltpu.CompilerParams(
            collective_id=0, has_side_effects=True, vmem_limit_bytes=63 * 1024 * 1024
        ),
        cost_estimate=pl.CostEstimate(
            flops=500_000_000, bytes_accessed=13_000_000, transcendentals=600_000
        ),
    )(
        queries, prefix_kv, suffix_kv, suffix_len, prefill_group, sampler_groups.T,
        out_weight, norm_gain, residual,
    )


def solution(mesh):
    in_specs = (
        P("grp", "tp"),
        P("grp", None, None, "tp"),
        P("grp", None, None, "tp"),
        P("grp"),
        P(),
        P(),
        P("tp", None),
        P("tp"),
        P("grp", "tp"),
    )
    return jax.shard_map(
        shards, mesh=mesh, in_specs=in_specs, out_specs=P("grp", "tp"), check_vma=False
    )
```

```python
import jax
import jax.numpy as jnp
from jax import lax
from jax.experimental import pallas as pl
from jax.experimental.pallas import tpu as pltpu
from jax.sharding import PartitionSpec as P

MESH = pl.DeviceIdType.MESH
D = 4608
HD = 128
SAMP = 16
SLOTS = 4
PREFIX = 1024
SUF = 32
HEADS = 8
KVHEADS = 4
COLS = 1152
PROMPTS = 64
SCORE_SCALE = 144.0 ** (-0.5)
NORM_EPS = 1e-06
NEG = -1e30

Z_FAR = (4, 3, 5, 2, 6, 1, 7)
Z_NEAR = (1, 7, 2, 6, 3, 5, 4)
B_FAR = ((2, 1), (1, 1), (3, 1), (2, 0), (0, 1), (1, 0), (3, 0))

f32 = jnp.float32
bf16 = jnp.bfloat16
i32 = jnp.int32


def kernel(
    q_hbm, kv_hbm, suf_hbm, len_hbm, pre_hbm, sam_hbm, w_hbm, gain_hbm, res_hbm,
    o_ref,
    qh, kv, suf, w, gain, res, len_s, pre_s, sam_s, sam_v,
    own_p, pick_s,
    qall, csend, qc, rsend, rc, bsend1, bsend2, bt1, bt2, asend, fin,
    hot, hot2, lmask, suf_o, suf_l, psend, pr, sqs, sqr,
    lq, lkv, lsuf, lw, lsmall, lint,
    sa, ra, sb, rb, sc, rcs, sct, rct, sbt, rbt, sat, rat, srs, rrs, ssq, rsq,
):
    me = lax.axis_index("grp")
    tp = lax.axis_index("tp")
    x = me // 16
    z = (me // 2) % 8
    yh = me % 2
    b = x * 2 + yh

    def grp_of(xx, zz, yy):
        return (xx * 8 + zz) * 2 + yy

    def z_peer(off):
        zz = (z + off) % 8
        return zz, (grp_of(x, zz, yh), tp)

    def b_peer(off):
        xx = (x + off[0]) % 4
        yy = (yh + off[1]) % 2
        return xx * 2 + yy, (grp_of(xx, z, yy), tp)

    def tp_peer(off):
        yy, cc = (tp // 2 + off // 2) % 2, (tp % 2 + off % 2) % 2
        return yy * 2 + cc, (me, yy * 2 + cc)

    def remote(src, dst, send, recv, device):
        return pltpu.make_async_remote_copy(
            src_ref=src, dst_ref=dst, send_sem=send, recv_sem=recv,
            device_id=device, device_id_type=MESH,
        )

    barrier = pltpu.get_barrier_semaphore()
    for off in Z_FAR:
        pl.semaphore_signal(barrier, inc=1, device_id=z_peer(off)[1], device_id_type=MESH)
    for off in B_FAR:
        pl.semaphore_signal(barrier, inc=1, device_id=b_peer(off)[1], device_id_type=MESH)
    for off in (2, 3, 1):
        pl.semaphore_signal(barrier, inc=1, device_id=tp_peer(off)[1], device_id_type=MESH)

    ints = [
        pltpu.make_async_copy(pre_hbm, pre_s, lint.at[0]),
        pltpu.make_async_copy(sam_hbm, sam_s, lint.at[1]),
        pltpu.make_async_copy(sam_hbm, sam_v, lint.at[2]),
        pltpu.make_async_copy(len_hbm, len_s, lint.at[3]),
    ]
    for copy in ints:
        copy.start()
    for i in range(HEADS):
        pltpu.make_async_copy(q_hbm.at[:, pl.ds(i * HD, HD)], qh.at[i], lq).start()
    for part in range(2):
        for k in range(KVHEADS):
            pltpu.make_async_copy(
                kv_hbm.at[0, part, :, pl.ds(k * HD, HD)], kv.at[part, k], lkv
            ).start()
    for part in range(2):
        for k in range(KVHEADS):
            pltpu.make_async_copy(
                suf_hbm.at[:, part, :, pl.ds(k * HD, HD)], suf.at[part, k], lsuf
            ).start()
    small = [
        pltpu.make_async_copy(gain_hbm, gain, lsmall.at[0]),
        pltpu.make_async_copy(res_hbm, res, lsmall.at[1]),
    ]
    for copy in small:
        copy.start()
    for t in range(4):
        pltpu.make_async_copy(w_hbm.at[:, pl.ds(t * COLS, COLS)], w.at[t], lw).start()

    for copy in ints:
        copy.wait()

    line = [z_peer(off)[1][0] for off in range(8)]

    def find(p, found):
        group = pre_s[p]
        return tuple(found[off] + jnp.where(group == line[off], p, 0) for off in range(8))

    found = lax.fori_loop(0, PROMPTS, find, (jnp.int32(0),) * 8)
    for off in range(8):
        own_p[off] = found[off]
        for s in range(SLOTS):
            pick_s[off * SLOTS + s] = sam_s[s, found[off] & 63]

    pltpu.make_async_copy(qh, qh, lq).wait()
    pl.semaphore_wait(barrier, 17)

    for off in Z_FAR:
        zz, device = z_peer(off)
        remote(qh.at[zz], qall.at[off], sa, ra.at[off], device).start()
    qall[0] = qh[z]

    for off in (0,) + Z_NEAR:
        block = qall.at[off]
        if off != 0:
            remote(qh.at[0], block, sa, ra.at[off], (me, tp)).wait_recv()
        for boff in B_FAR:
            slot = (boff[0] * 2 + boff[1]) * 8 + off
            remote(block, qall.at[slot], sb, rb, b_peer(boff)[1]).start()
    others = qall.at[pl.ds(8, 56)]
    remote(others, others, sb, rb, (me, tp)).wait_recv()

    for off in Z_FAR + (0,):
        for s in range(SLOTS):
            g = pick_s[off * SLOTS + s]
            slot = (((x - (g >> 4)) & 3) * 2 + ((yh - g) & 1)) * 8 + ((z - (g >> 1)) & 7)
            block = qall[slot]
            if off == 0:
                qc[0, pl.ds(s * SAMP, SAMP)] = block
            else:
                csend[off, pl.ds(s * SAMP, SAMP)] = block
        if off != 0:
            remote(csend.at[off], qc.at[off], sc, rcs.at[off], z_peer(off)[1]).start()

    lane = lax.broadcasted_iota(i32, (1, 512), 1)
    lane_block = lane >> 4
    lane_row = lane & 15
    group_lane = jnp.zeros((1, 512), i32)
    prompt_lane = jnp.zeros((1, 512), i32)
    for c in range(32):
        group_lane = jnp.where(lane_block == c, pick_s[c], group_lane)
    for off in range(8):
        prompt_lane = jnp.where((lane >> 6) == off, own_p[off], prompt_lane)
    pick_b = (((group_lane >> 4) - x) & 3) * 2 + ((group_lane - yh) & 1)
    pick_z = ((group_lane >> 1) - z) & 7
    table = jnp.transpose(sam_v[...])
    member = jnp.zeros((PROMPTS, 512), f32)
    for s in range(SLOTS):
        member = member + jnp.where(table[:, s : s + 1] == group_lane, 1.0, 0.0)
    prompt_row = lax.broadcasted_iota(i32, (PROMPTS, 512), 0)
    count = jnp.sum(member, axis=0, keepdims=True)
    rank = jnp.sum(jnp.where(prompt_row < prompt_lane, member, 0.0), axis=0, keepdims=True)
    row = lane_row.astype(f32)
    rest = row - jnp.floor((row + 0.5) / count) * count
    owned = rest == rank
    place = jnp.where(owned, (pick_b * 8 + pick_z) * SAMP + lane_row, -1)
    place2 = jnp.where(owned, pick_b * SAMP + lane_row, -1)
    few = lax.broadcasted_iota(i32, (SAMP, 512), 0)
    for n in range(8):
        for at, off in enumerate(Z_FAR + (0,)):
            row_of = few + (n * 8 + off) * SAMP
            hot[n, pl.ds(at * SAMP, SAMP)] = jnp.where(row_of == place, 1.0, 0.0).astype(bf16)
    rows = lax.broadcasted_iota(i32, (128, 512), 0)
    hot2[...] = jnp.where(rows == place2, 1.0, 0.0).astype(bf16)
    tile_lane = lax.broadcasted_iota(i32, (SAMP, HD), 1)
    for c in range(32):
        of_z = ((pick_s[c] >> 1) - z) & 7
        keep = ((tile_lane >> 3) == of_z) & (((tile_lane & 7) >> 1) == c % SLOTS)
        lmask[pl.ds(c * SAMP, SAMP)] = jnp.where(keep, 1.0, 0.0).astype(bf16)

    pltpu.make_async_copy(kv, kv, lkv).wait()

    def attend(off):
        k = z_peer(-off)[0] // 2
        scores = (
            lax.dot_general(
                qc[off], kv[0, k], (((1,), (1,)), ((), ())), preferred_element_type=f32
            )
            * SCORE_SCALE
        )
        top = jnp.max(scores, axis=1, keepdims=True)
        weights = jnp.exp(scores - top)
        total = jnp.sum(weights, axis=1, keepdims=True)
        out = jnp.dot(weights.astype(bf16), kv[1, k], preferred_element_type=f32) / total
        log_total = top + jnp.log(total)
        high = log_total.astype(bf16).astype(f32)
        low = log_total - high
        tile = jnp.zeros((SAMP, HD), f32)
        for s in range(SLOTS):
            at = s * SAMP
            tile = jnp.where((tile_lane & 7) == 2 * s, high[at : at + SAMP], tile)
            tile = jnp.where((tile_lane & 7) == 2 * s + 1, low[at : at + SAMP], tile)
        return out.astype(bf16), tile.astype(bf16)

    for group in ((0,), (1, 7), (2, 6), (4,), (3, 5)):
        for off in group:
            if off != 0:
                remote(csend.at[off], qc.at[off], sc, rcs.at[off], (me, tp)).wait_recv()
        results = [attend(off) for off in group]
        for off, (out, tile) in zip(group, results):
            result = rc if off == 0 else rsend
            result[off, pl.ds(0, 64)] = out
            result[off, pl.ds(64, SAMP)] = tile
            if off != 0:
                remote(
                    rsend.at[off], rc.at[off], sct, rct, z_peer(-off)[1]
                ).start()

    pltpu.make_async_copy(suf, suf, lsuf).wait()
    col = lax.broadcasted_iota(i32, (32, 512), 1)
    srow = lax.broadcasted_iota(i32, (32, 512), 0) & 15
    col_sample = col >> 5
    live_len = jnp.zeros((32, 512), i32)
    for s in range(SAMP):
        live_len = jnp.where(col_sample == s, len_s[s], live_len)
    live = (col_sample == srow) & ((col & 31) < live_len)
    for k in range(KVHEADS):
        query = qh[pl.ds(2 * k, 2)].reshape(32, HD)
        scores = (
            lax.dot_general(
                query, suf[0, k].reshape(512, HD), (((1,), (1,)), ((), ())),
                preferred_element_type=f32,
            )
            * SCORE_SCALE
        )
        top = jnp.max(jnp.where(live, scores, NEG), axis=1, keepdims=True)
        weights = jnp.where(live, jnp.exp(jnp.where(live, scores - top, 0.0)), 0.0)
        total = jnp.sum(weights, axis=1, keepdims=True)
        out = (
            jnp.dot(weights.astype(bf16), suf[1, k].reshape(512, HD), preferred_element_type=f32)
            / total
        )
        suf_o[pl.ds(k * 32, 32)] = out
        suf_l[pl.ds(k * 32, 32)] = jnp.broadcast_to(top + jnp.log(total), (32, HD))

    seven = rc.at[pl.ds(1, 7)]
    remote(seven, seven, sct, rct, (me, tp)).wait_recv()
    results = rc[:, pl.ds(0, 64)].reshape(512, HD)
    logs = jnp.concatenate(
        [rc[off, pl.ds(64, SAMP)] for off in range(8) for _ in range(SLOTS)], axis=0
    ) * lmask[...]
    log_rows = jnp.dot(hot2[...], logs, preferred_element_type=f32).astype(bf16)

    for boff in B_FAR + ((0, 0),):
        n = boff[0] * 2 + boff[1]
        picked = jnp.dot(hot[n], results, preferred_element_type=f32).astype(bf16)
        first, second = (bt1, bt2) if n == 0 else (bsend1, bsend2)
        first[n, pl.ds(0, 48)] = picked[:48]
        first[n, pl.ds(48, SAMP)] = log_rows[n * SAMP : (n + 1) * SAMP]
        second[n] = picked[48:]
        if n != 0:
            remote(bsend1.at[n], bt1.at[n], sbt.at[0], rbt.at[0], b_peer(boff)[1]).start()
    for boff in B_FAR:
        n = boff[0] * 2 + boff[1]
        remote(bsend2.at[n], bt2.at[n], sbt.at[1], rbt.at[1], b_peer(boff)[1]).start()

    def merge(ref):
        merged = ref[0].astype(f32)
        for n in range(1, 8):
            merged = merged + ref[n].astype(f32)
        return merged.astype(bf16)

    def give(off, block, logs):
        ref = fin if off == 0 else asend
        ref[off, pl.ds(0, SAMP)] = block
        ref[off, pl.ds(SAMP, SAMP)] = logs
        if off != 0:
            remote(asend.at[off], fin.at[off], sat, rat, z_peer(off)[1]).start()

    seven = bt1.at[pl.ds(1, 7)]
    remote(seven, seven, sbt.at[0], rbt.at[0], (me, tp)).wait_recv()
    merged = merge(bt1)
    logs = merged[48:]
    for at, off in enumerate(Z_FAR[:3]):
        give(off, merged[at * SAMP : (at + 1) * SAMP], logs)
    seven = bt2.at[pl.ds(1, 7)]
    remote(seven, seven, sbt.at[1], rbt.at[1], (me, tp)).wait_recv()
    merged = merge(bt2)
    for at, off in enumerate(Z_FAR[3:] + (0,)):
        give(off, merged[at * SAMP : (at + 1) * SAMP], logs)
    pltpu.make_async_copy(w, w, lw).wait()
    seven = fin.at[pl.ds(1, 7)]
    remote(seven, seven, sat, rat, (me, tp)).wait_recv()

    come = [fin[(z - i) % 8] for i in range(HEADS)]
    prefix_out = jnp.concatenate([block[:SAMP] for block in come], axis=0).astype(f32)
    log_tile = jnp.concatenate([block[SAMP:] for block in come], axis=0).astype(f32)
    all_lane = lax.broadcasted_iota(i32, (128, HD), 1)
    all_row = lax.broadcasted_iota(i32, (128, HD), 0)
    prefix_log = jnp.sum(
        jnp.where((all_lane >> 3) == ((z - (all_row >> 4)) & 7), log_tile, 0.0),
        axis=1, keepdims=True,
    )
    suffix_log = suf_l[...]
    joint = jnp.maximum(prefix_log, suffix_log)
    share_p = jnp.exp(prefix_log - joint)
    share_s = jnp.exp(suffix_log - joint)
    attended = (
        (share_p * prefix_out + share_s * suf_o[...]) / (share_p + share_s)
    ).astype(bf16)
    attended = jnp.concatenate(
        [attended[i * SAMP : (i + 1) * SAMP] for i in range(HEADS)], axis=1
    )

    for off in (2, 3, 1):
        tt, device = tp_peer(off)
        psend[off - 1] = jnp.dot(attended, w[tt], preferred_element_type=f32).astype(bf16)
        remote(psend.at[off - 1], pr.at[off - 1], srs, rrs, device).start()
    projected = jnp.dot(attended, w[tp], preferred_element_type=f32)
    remote(psend, pr, srs, rrs, (me, tp)).wait_recv()
    for off in range(3):
        projected = projected + pr[off].astype(f32)
    squares = jnp.zeros((SAMP, HD), f32)
    for n in range(COLS // HD):
        piece = projected[:, n * HD : (n + 1) * HD]
        squares = squares + piece * piece
    sqs[...] = squares
    for off in (2, 3, 1):
        remote(sqs, sqr.at[off - 1], ssq.at[off - 1], rsq, tp_peer(off)[1]).start()
    for copy in small:
        copy.wait()
    remote(sqr, sqr, ssq.at[0], rsq, (me, tp)).wait_recv()
    for off in range(3):
        squares = squares + sqr[off]
    scale = lax.rsqrt(jnp.sum(squares, axis=1, keepdims=True) / D + NORM_EPS)
    o_ref[...] = (res[...].astype(f32) + projected * scale * gain[...].reshape(1, COLS)).astype(bf16)

    seven = qall.at[pl.ds(0, 7)]
    remote(seven, seven, sa, ra.at[0], (me, tp)).wait_send()
    seven = qall.at[pl.ds(0, 56)]
    remote(seven, seven, sb, rb, (me, tp)).wait_send()
    for ref, send, recv in (
        (csend, sc, rcs.at[0]), (rc, sct, rct), (bt1, sbt.at[0], rbt.at[0]),
        (bt2, sbt.at[1], rbt.at[1]), (fin, sat, rat),
    ):
        seven = ref.at[pl.ds(0, 7)]
        remote(seven, seven, send, recv, (me, tp)).wait_send()
    remote(psend, pr, srs, rrs, (me, tp)).wait_send()
    for off in range(3):
        remote(sqs, sqr.at[off], ssq.at[off], rsq, (me, tp)).wait_send()


def shards(
    queries, prefix_kv, suffix_kv, suffix_len, prefill_group, sampler_groups,
    out_weight, norm_gain, residual,
):
    vmem = pltpu.VMEM
    dma = pltpu.SemaphoreType.DMA
    scratch = [
        vmem((HEADS, SAMP, HD), bf16),
        vmem((2, KVHEADS, PREFIX, HD), bf16),
        vmem((2, KVHEADS, SAMP, SUF, HD), bf16),
        vmem((4, HEADS * HD, COLS), bf16),
        vmem((COLS,), f32),
        vmem((SAMP, COLS), bf16),
        pltpu.SMEM((SAMP,), i32),
        pltpu.SMEM((PROMPTS,), i32),
        pltpu.SMEM((SLOTS, PROMPTS), i32),
        vmem((SLOTS, PROMPTS), i32),
        pltpu.SMEM((8,), i32),
        pltpu.SMEM((32,), i32),
        vmem((64, SAMP, HD), bf16),
        vmem((8, 64, HD), bf16),
        vmem((8, 64, HD), bf16),
        vmem((8, 80, HD), bf16),
        vmem((8, 80, HD), bf16),
        vmem((8, 64, HD), bf16),
        vmem((8, 80, HD), bf16),
        vmem((8, 64, HD), bf16),
        vmem((8, 80, HD), bf16),
        vmem((8, 32, HD), bf16),
        vmem((8, 32, HD), bf16),
        vmem((8, 128, 512), bf16),
        vmem((128, 512), bf16),
        vmem((512, HD), bf16),
        vmem((128, HD), f32),
        vmem((128, HD), f32),
        vmem((3, SAMP, COLS), bf16),
        vmem((3, SAMP, COLS), bf16),
        vmem((SAMP, HD), f32),
        vmem((3, SAMP, HD), f32),
        dma, dma, dma, dma, dma((2,)), dma((4,)),
        dma, dma((8,)),
        dma, dma,
        dma, dma((8,)),
        dma, dma,
        dma((2,)), dma((2,)),
        dma, dma,
        dma, dma,
        dma((3,)), dma,
    ]
    anywhere = pl.BlockSpec(memory_space=pl.ANY)
    return pl.pallas_call(
        kernel,
        out_shape=jax.ShapeDtypeStruct(residual.shape, bf16),
        in_specs=[anywhere] * 9,
        out_specs=pl.BlockSpec(memory_space=pltpu.VMEM),
        scratch_shapes=scratch,
        compiler_params=pltpu.CompilerParams(
            collective_id=0, has_side_effects=True, vmem_limit_bytes=63 * 1024 * 1024
        ),
        cost_estimate=pl.CostEstimate(
            flops=500_000_000, bytes_accessed=13_000_000, transcendentals=600_000
        ),
    )(
        queries, prefix_kv, suffix_kv, suffix_len, prefill_group, sampler_groups.T,
        out_weight, norm_gain, residual,
    )


def solution(mesh):
    in_specs = (
        P("grp", "tp"),
        P("grp", None, None, "tp"),
        P("grp", None, None, "tp"),
        P("grp"),
        P(),
        P(),
        P("tp", None),
        P("tp"),
        P("grp", "tp"),
    )
    return jax.shard_map(
        shards, mesh=mesh, in_specs=in_specs, out_specs=P("grp", "tp"), check_vma=False
    )
```

```python
import jax
import jax.numpy as jnp
from jax import lax
from jax.experimental import pallas as pl
from jax.experimental.pallas import tpu as pltpu
from jax.sharding import PartitionSpec as P

MESH = pl.DeviceIdType.MESH
D = 4608
HD = 128
SAMP = 16
SLOTS = 4
PREFIX = 1024
SUF = 32
HEADS = 8
KVHEADS = 4
COLS = 1152
PROMPTS = 64
SCORE_SCALE = 144.0 ** (-0.5)
NORM_EPS = 1e-06
NEG = -1e30

Z_FAR = (4, 3, 5, 2, 6, 1, 7)
Z_NEAR = (1, 7, 2, 6, 3, 5, 4)
B_FAR = ((2, 1), (1, 1), (3, 1), (2, 0), (0, 1), (1, 0), (3, 0))

f32 = jnp.float32
bf16 = jnp.bfloat16
i32 = jnp.int32


def kernel(
    q_hbm, kv_hbm, suf_hbm, len_hbm, pre_hbm, sam_hbm, w_hbm, gain_hbm, res_hbm,
    o_ref,
    qh, kv, suf, w, gain, res, len_s, pre_s, sam_s, sam_v,
    own_p, pick_s,
    qall, csend, qc, rsend, rc, bsend1, bsend2, bt1, bt2, asend, fin,
    hot1, hot2, lmask, suf_o, suf_l, psend, pr, sqs, sqr,
    lq, lkv, lsuf, lw, lsmall, lint,
    sa, ra, sb, rb, sc, rcs, sct, rct, sbt, rbt, sat, rat, srs, rrs, ssq, rsq,
):
    me = lax.axis_index("grp")
    tp = lax.axis_index("tp")
    x = me // 16
    z = (me // 2) % 8
    yh = me % 2
    b = x * 2 + yh

    def grp_of(xx, zz, yy):
        return (xx * 8 + zz) * 2 + yy

    def z_peer(off):
        zz = (z + off) % 8
        return zz, (grp_of(x, zz, yh), tp)

    def b_peer(off):
        xx = (x + off[0]) % 4
        yy = (yh + off[1]) % 2
        return xx * 2 + yy, (grp_of(xx, z, yy), tp)

    def tp_peer(off):
        yy, cc = (tp // 2 + off // 2) % 2, (tp % 2 + off % 2) % 2
        return yy * 2 + cc, (me, yy * 2 + cc)

    def remote(src, dst, send, recv, device):
        return pltpu.make_async_remote_copy(
            src_ref=src, dst_ref=dst, send_sem=send, recv_sem=recv,
            device_id=device, device_id_type=MESH,
        )

    barrier = pltpu.get_barrier_semaphore()
    for off in Z_FAR:
        pl.semaphore_signal(barrier, inc=1, device_id=z_peer(off)[1], device_id_type=MESH)
    for off in B_FAR:
        pl.semaphore_signal(barrier, inc=1, device_id=b_peer(off)[1], device_id_type=MESH)
    for off in (2, 3, 1):
        pl.semaphore_signal(barrier, inc=1, device_id=tp_peer(off)[1], device_id_type=MESH)

    ints = [
        pltpu.make_async_copy(pre_hbm, pre_s, lint.at[0]),
        pltpu.make_async_copy(sam_hbm, sam_s, lint.at[1]),
        pltpu.make_async_copy(sam_hbm, sam_v, lint.at[2]),
        pltpu.make_async_copy(len_hbm, len_s, lint.at[3]),
    ]
    for copy in ints:
        copy.start()
    for i in range(HEADS):
        pltpu.make_async_copy(q_hbm.at[:, pl.ds(i * HD, HD)], qh.at[i], lq).start()
    for part in range(2):
        for k in range(KVHEADS):
            pltpu.make_async_copy(
                kv_hbm.at[0, part, :, pl.ds(k * HD, HD)], kv.at[part, k], lkv
            ).start()
    for part in range(2):
        for k in range(KVHEADS):
            pltpu.make_async_copy(
                suf_hbm.at[:, part, :, pl.ds(k * HD, HD)], suf.at[part, k], lsuf
            ).start()
    small = [
        pltpu.make_async_copy(gain_hbm, gain, lsmall.at[0]),
        pltpu.make_async_copy(res_hbm, res, lsmall.at[1]),
    ]
    for copy in small:
        copy.start()
    for t in range(4):
        pltpu.make_async_copy(w_hbm.at[:, pl.ds(t * COLS, COLS)], w.at[t], lw).start()

    for copy in ints:
        copy.wait()

    line = [z_peer(off)[1][0] for off in range(8)]

    def find(p, found):
        group = pre_s[p]
        return tuple(found[off] + jnp.where(group == line[off], p, 0) for off in range(8))

    found = lax.fori_loop(0, PROMPTS, find, (jnp.int32(0),) * 8)
    for off in range(8):
        own_p[off] = found[off]
        for s in range(SLOTS):
            pick_s[off * SLOTS + s] = sam_s[s, found[off] & 63]

    pltpu.make_async_copy(qh, qh, lq).wait()
    pl.semaphore_wait(barrier, 17)

    for off in Z_FAR:
        zz, device = z_peer(off)
        remote(qh.at[zz], qall.at[off], sa, ra.at[off], device).start()
    qall[0] = qh[z]

    for off in (0,) + Z_NEAR:
        block = qall.at[off]
        if off != 0:
            remote(qh.at[0], block, sa, ra.at[off], (me, tp)).wait_recv()
        for boff in B_FAR:
            slot = (boff[0] * 2 + boff[1]) * 8 + off
            remote(block, qall.at[slot], sb, rb, b_peer(boff)[1]).start()
    others = qall.at[pl.ds(8, 56)]
    remote(others, others, sb, rb, (me, tp)).wait_recv()

    for off in Z_FAR + (0,):
        for s in range(SLOTS):
            g = pick_s[off * SLOTS + s]
            slot = (((x - (g >> 4)) & 3) * 2 + ((yh - g) & 1)) * 8 + ((z - (g >> 1)) & 7)
            block = qall[slot]
            if off == 0:
                qc[0, pl.ds(s * SAMP, SAMP)] = block
            else:
                csend[off, pl.ds(s * SAMP, SAMP)] = block
        if off != 0:
            remote(csend.at[off], qc.at[off], sc, rcs.at[off], z_peer(off)[1]).start()

    lane = lax.broadcasted_iota(i32, (1, 512), 1)
    lane_block = lane >> 4
    lane_row = lane & 15
    group_lane = jnp.zeros((1, 512), i32)
    prompt_lane = jnp.zeros((1, 512), i32)
    for c in range(32):
        group_lane = jnp.where(lane_block == c, pick_s[c], group_lane)
    for off in range(8):
        prompt_lane = jnp.where((lane >> 6) == off, own_p[off], prompt_lane)
    pick_b = (((group_lane >> 4) - x) & 3) * 2 + ((group_lane - yh) & 1)
    pick_z = ((group_lane >> 1) - z) & 7
    table = jnp.transpose(sam_v[...])
    member = jnp.zeros((PROMPTS, 512), f32)
    for s in range(SLOTS):
        member = member + jnp.where(table[:, s : s + 1] == group_lane, 1.0, 0.0)
    prompt_row = lax.broadcasted_iota(i32, (PROMPTS, 512), 0)
    count = jnp.sum(member, axis=0, keepdims=True)
    rank = jnp.sum(jnp.where(prompt_row < prompt_lane, member, 0.0), axis=0, keepdims=True)
    row = lane_row.astype(f32)
    rest = row - jnp.floor((row + 0.5) / count) * count
    owned = rest == rank
    place = jnp.where(owned, (pick_b * 8 + pick_z) * SAMP + lane_row, -1)
    place2 = jnp.where(owned, pick_b * SAMP + lane_row, -1)
    few = lax.broadcasted_iota(i32, (SAMP, 512), 0)

    def one_hot(first, wanted):
        return jnp.where(few + first * SAMP == wanted, 1.0, 0.0).astype(bf16)

    for n in range(8):
        for at, off in enumerate(Z_FAR[:3]):
            hot1[n, pl.ds(at * SAMP, SAMP)] = one_hot(n * 8 + off, place)
        hot1[n, pl.ds(48, SAMP)] = one_hot(n, place2)
        for at, off in enumerate(Z_FAR[3:] + (0,)):
            hot2[n, pl.ds(at * SAMP, SAMP)] = one_hot(n * 8 + off, place)
    tile_lane = lax.broadcasted_iota(i32, (SAMP, HD), 1)
    for c in range(32):
        of_z = ((pick_s[c] >> 1) - z) & 7
        keep = ((tile_lane >> 3) == of_z) & (((tile_lane & 7) >> 1) == c % SLOTS)
        lmask[pl.ds(c * SAMP, SAMP)] = jnp.where(keep, 1.0, 0.0).astype(bf16)

    pltpu.make_async_copy(kv, kv, lkv).wait()

    def attend(off):
        k = z_peer(-off)[0] // 2
        scores = (
            lax.dot_general(
                qc[off], kv[0, k], (((1,), (1,)), ((), ())), preferred_element_type=f32
            )
            * SCORE_SCALE
        )
        top = jnp.max(scores, axis=1, keepdims=True)
        weights = jnp.exp(scores - top)
        total = jnp.sum(weights, axis=1, keepdims=True)
        out = jnp.dot(weights.astype(bf16), kv[1, k], preferred_element_type=f32) / total
        log_total = top + jnp.log(total)
        high = log_total.astype(bf16).astype(f32)
        low = log_total - high
        tile = jnp.zeros((SAMP, HD), f32)
        for s in range(SLOTS):
            at = s * SAMP
            tile = jnp.where((tile_lane & 7) == 2 * s, high[at : at + SAMP], tile)
            tile = jnp.where((tile_lane & 7) == 2 * s + 1, low[at : at + SAMP], tile)
        return out.astype(bf16), tile.astype(bf16)

    for group in ((4,), (3, 5), (2, 6), (1, 7), (0,)):
        for off in group:
            if off != 0:
                remote(csend.at[off], qc.at[off], sc, rcs.at[off], (me, tp)).wait_recv()
        results = [attend(off) for off in group]
        for off, (out, tile) in zip(group, results):
            result = rc if off == 0 else rsend
            result[off, pl.ds(0, 64)] = out
            result[off, pl.ds(64, SAMP)] = tile
            if off != 0:
                remote(
                    rsend.at[off], rc.at[off], sct, rct, z_peer(-off)[1]
                ).start()

    pltpu.make_async_copy(suf, suf, lsuf).wait()
    col = lax.broadcasted_iota(i32, (32, 512), 1)
    srow = lax.broadcasted_iota(i32, (32, 512), 0) & 15
    col_sample = col >> 5
    live_len = jnp.zeros((32, 512), i32)
    for s in range(SAMP):
        live_len = jnp.where(col_sample == s, len_s[s], live_len)
    live = (col_sample == srow) & ((col & 31) < live_len)
    for k in range(KVHEADS):
        query = qh[pl.ds(2 * k, 2)].reshape(32, HD)
        scores = (
            lax.dot_general(
                query, suf[0, k].reshape(512, HD), (((1,), (1,)), ((), ())),
                preferred_element_type=f32,
            )
            * SCORE_SCALE
        )
        top = jnp.max(jnp.where(live, scores, NEG), axis=1, keepdims=True)
        weights = jnp.where(live, jnp.exp(jnp.where(live, scores - top, 0.0)), 0.0)
        total = jnp.sum(weights, axis=1, keepdims=True)
        out = (
            jnp.dot(weights.astype(bf16), suf[1, k].reshape(512, HD), preferred_element_type=f32)
            / total
        )
        suf_o[pl.ds(k * 32, 32)] = out
        suf_l[pl.ds(k * 32, 32)] = jnp.broadcast_to(top + jnp.log(total), (32, HD))

    seven = rc.at[pl.ds(1, 7)]
    remote(seven, seven, sct, rct, (me, tp)).wait_recv()
    results = rc[:, pl.ds(0, 64)].reshape(512, HD)
    logs = jnp.concatenate(
        [rc[off, pl.ds(64, SAMP)] for off in range(8) for _ in range(SLOTS)], axis=0
    ) * lmask[...]
    both = jnp.concatenate([results, logs], axis=1)

    def from_b(boff):
        n = boff[0] * 2 + boff[1]
        first, second = (bt1, bt2) if n == 0 else (bsend1, bsend2)
        return n, first.at[n], second.at[n]

    for boff in B_FAR + ((0, 0),):
        n, first, _ = from_b(boff)
        picked = jnp.dot(hot1[n], both, preferred_element_type=f32).astype(bf16)
        first[pl.ds(0, 48)] = picked[:48, :HD]
        first[pl.ds(48, SAMP)] = picked[48:, HD:]
        if n != 0:
            remote(first, bt1.at[n], sbt.at[0], rbt.at[0], b_peer(boff)[1]).start()
    for boff in B_FAR + ((0, 0),):
        n, _, second = from_b(boff)
        second[...] = jnp.dot(hot2[n], results, preferred_element_type=f32).astype(bf16)
        if n != 0:
            remote(second, bt2.at[n], sbt.at[1], rbt.at[1], b_peer(boff)[1]).start()

    def merge(ref):
        merged = ref[0].astype(f32)
        for n in range(1, 8):
            merged = merged + ref[n].astype(f32)
        return merged.astype(bf16)

    def give(off, block, logs):
        ref = fin if off == 0 else asend
        ref[off, pl.ds(0, SAMP)] = block
        ref[off, pl.ds(SAMP, SAMP)] = logs
        if off != 0:
            remote(asend.at[off], fin.at[off], sat, rat, z_peer(off)[1]).start()

    seven = bt1.at[pl.ds(1, 7)]
    remote(seven, seven, sbt.at[0], rbt.at[0], (me, tp)).wait_recv()
    merged = merge(bt1)
    logs = merged[48:]
    for at, off in enumerate(Z_FAR[:3]):
        give(off, merged[at * SAMP : (at + 1) * SAMP], logs)
    seven = bt2.at[pl.ds(1, 7)]
    remote(seven, seven, sbt.at[1], rbt.at[1], (me, tp)).wait_recv()
    merged = merge(bt2)
    for at, off in enumerate(Z_FAR[3:] + (0,)):
        give(off, merged[at * SAMP : (at + 1) * SAMP], logs)
    pltpu.make_async_copy(w, w, lw).wait()
    seven = fin.at[pl.ds(1, 7)]
    remote(seven, seven, sat, rat, (me, tp)).wait_recv()

    come = [fin[(z - i) % 8] for i in range(HEADS)]
    prefix_out = jnp.concatenate([block[:SAMP] for block in come], axis=0).astype(f32)
    log_tile = jnp.concatenate([block[SAMP:] for block in come], axis=0).astype(f32)
    all_lane = lax.broadcasted_iota(i32, (128, HD), 1)
    all_row = lax.broadcasted_iota(i32, (128, HD), 0)
    prefix_log = jnp.sum(
        jnp.where((all_lane >> 3) == ((z - (all_row >> 4)) & 7), log_tile, 0.0),
        axis=1, keepdims=True,
    )
    suffix_log = suf_l[...]
    joint = jnp.maximum(prefix_log, suffix_log)
    share_p = jnp.exp(prefix_log - joint)
    share_s = jnp.exp(suffix_log - joint)
    attended = (
        (share_p * prefix_out + share_s * suf_o[...]) / (share_p + share_s)
    ).astype(bf16)
    attended = jnp.concatenate(
        [attended[i * SAMP : (i + 1) * SAMP] for i in range(HEADS)], axis=1
    )

    for off in (2, 3, 1):
        tt, device = tp_peer(off)
        psend[off - 1] = jnp.dot(attended, w[tt], preferred_element_type=f32).astype(bf16)
        remote(psend.at[off - 1], pr.at[off - 1], srs, rrs, device).start()
    projected = jnp.dot(attended, w[tp], preferred_element_type=f32)
    remote(psend, pr, srs, rrs, (me, tp)).wait_recv()
    for off in range(3):
        projected = projected + pr[off].astype(f32)
    squares = jnp.zeros((SAMP, HD), f32)
    for n in range(COLS // HD):
        piece = projected[:, n * HD : (n + 1) * HD]
        squares = squares + piece * piece
    sqs[...] = squares
    for off in (2, 3, 1):
        remote(sqs, sqr.at[off - 1], ssq.at[off - 1], rsq, tp_peer(off)[1]).start()
    for copy in small:
        copy.wait()
    remote(sqr, sqr, ssq.at[0], rsq, (me, tp)).wait_recv()
    for off in range(3):
        squares = squares + sqr[off]
    scale = lax.rsqrt(jnp.sum(squares, axis=1, keepdims=True) / D + NORM_EPS)
    o_ref[...] = (res[...].astype(f32) + projected * scale * gain[...].reshape(1, COLS)).astype(bf16)

    seven = qall.at[pl.ds(0, 7)]
    remote(seven, seven, sa, ra.at[0], (me, tp)).wait_send()
    seven = qall.at[pl.ds(0, 56)]
    remote(seven, seven, sb, rb, (me, tp)).wait_send()
    for ref, send, recv in (
        (csend, sc, rcs.at[0]), (rc, sct, rct), (bt1, sbt.at[0], rbt.at[0]),
        (bt2, sbt.at[1], rbt.at[1]), (fin, sat, rat),
    ):
        seven = ref.at[pl.ds(0, 7)]
        remote(seven, seven, send, recv, (me, tp)).wait_send()
    remote(psend, pr, srs, rrs, (me, tp)).wait_send()
    for off in range(3):
        remote(sqs, sqr.at[off], ssq.at[off], rsq, (me, tp)).wait_send()


def shards(
    queries, prefix_kv, suffix_kv, suffix_len, prefill_group, sampler_groups,
    out_weight, norm_gain, residual,
):
    vmem = pltpu.VMEM
    dma = pltpu.SemaphoreType.DMA
    scratch = [
        vmem((HEADS, SAMP, HD), bf16),
        vmem((2, KVHEADS, PREFIX, HD), bf16),
        vmem((2, KVHEADS, SAMP, SUF, HD), bf16),
        vmem((4, HEADS * HD, COLS), bf16),
        vmem((COLS,), f32),
        vmem((SAMP, COLS), bf16),
        pltpu.SMEM((SAMP,), i32),
        pltpu.SMEM((PROMPTS,), i32),
        pltpu.SMEM((SLOTS, PROMPTS), i32),
        vmem((SLOTS, PROMPTS), i32),
        pltpu.SMEM((8,), i32),
        pltpu.SMEM((32,), i32),
        vmem((64, SAMP, HD), bf16),
        vmem((8, 64, HD), bf16),
        vmem((8, 64, HD), bf16),
        vmem((8, 80, HD), bf16),
        vmem((8, 80, HD), bf16),
        vmem((8, 64, HD), bf16),
        vmem((8, 80, HD), bf16),
        vmem((8, 64, HD), bf16),
        vmem((8, 80, HD), bf16),
        vmem((8, 32, HD), bf16),
        vmem((8, 32, HD), bf16),
        vmem((8, 64, 512), bf16),
        vmem((8, 80, 512), bf16),
        vmem((512, HD), bf16),
        vmem((128, HD), f32),
        vmem((128, HD), f32),
        vmem((3, SAMP, COLS), bf16),
        vmem((3, SAMP, COLS), bf16),
        vmem((SAMP, HD), f32),
        vmem((3, SAMP, HD), f32),
        dma, dma, dma, dma, dma((2,)), dma((4,)),
        dma, dma((8,)),
        dma, dma,
        dma, dma((8,)),
        dma, dma,
        dma((2,)), dma((2,)),
        dma, dma,
        dma, dma,
        dma((3,)), dma,
    ]
    anywhere = pl.BlockSpec(memory_space=pl.ANY)
    return pl.pallas_call(
        kernel,
        out_shape=jax.ShapeDtypeStruct(residual.shape, bf16),
        in_specs=[anywhere] * 9,
        out_specs=pl.BlockSpec(memory_space=pltpu.VMEM),
        scratch_shapes=scratch,
        compiler_params=pltpu.CompilerParams(
            collective_id=0, has_side_effects=True, vmem_limit_bytes=63 * 1024 * 1024
        ),
        cost_estimate=pl.CostEstimate(
            flops=500_000_000, bytes_accessed=13_000_000, transcendentals=600_000
        ),
    )(
        queries, prefix_kv, suffix_kv, suffix_len, prefill_group, sampler_groups.T,
        out_weight, norm_gain, residual,
    )


def solution(mesh):
    in_specs = (
        P("grp", "tp"),
        P("grp", None, None, "tp"),
        P("grp", None, None, "tp"),
        P("grp"),
        P(),
        P(),
        P("tp", None),
        P("tp"),
        P("grp", "tp"),
    )
    return jax.shard_map(
        shards, mesh=mesh, in_specs=in_specs, out_specs=P("grp", "tp"), check_vma=False
    )
```

```python
import jax
import jax.numpy as jnp
from jax import lax
from jax.experimental import pallas as pl
from jax.experimental.pallas import tpu as pltpu
from jax.sharding import PartitionSpec as P

MESH = pl.DeviceIdType.MESH
D = 4608
HD = 128
SAMP = 16
SLOTS = 4
PREFIX = 1024
SUF = 32
HEADS = 8
KVHEADS = 4
COLS = 1152
PROMPTS = 64
SCORE_SCALE = 144.0 ** (-0.5)
NORM_EPS = 1e-06
NEG = -1e30

Z_FAR = (4, 3, 5, 2, 6, 1, 7)
Z_NEAR = (1, 7, 2, 6, 3, 5, 4)
B_FAR = ((2, 1), (1, 1), (3, 1), (2, 0), (0, 1), (1, 0), (3, 0))

f32 = jnp.float32
bf16 = jnp.bfloat16
i32 = jnp.int32


def kernel(
    q_hbm, kv_hbm, suf_hbm, len_hbm, pre_hbm, sam_hbm, w_hbm, gain_hbm, res_hbm,
    o_ref,
    qh, kv, suf, w, gain, res, len_s, pre_s, sam_s, sam_v,
    own_p, pick_s,
    qall, csend, qc, rsend, rc, bsend1, bsend2, bt1, bt2, asend, fin,
    hot1, hot2, lmask, sxs, sx, psend, pr, sqs, sqr,
    lq, lkv, lsuf, lw, lsmall, lint,
    sa, ra, sb, rb, sc, rcs, sct, rct, sbt, rbt, sat, rat, srs, rrs, ssq, rsq, sw, rw, ssx, rsx,
):
    me = lax.axis_index("grp")
    tp = lax.axis_index("tp")
    x = me // 16
    z = (me // 2) % 8
    yh = me % 2
    b = x * 2 + yh

    def grp_of(xx, zz, yy):
        return (xx * 8 + zz) * 2 + yy

    def z_peer(off):
        zz = (z + off) % 8
        return zz, (grp_of(x, zz, yh), tp)

    def b_peer(off):
        xx = (x + off[0]) % 4
        yy = (yh + off[1]) % 2
        return xx * 2 + yy, (grp_of(xx, z, yy), tp)

    chip, core = tp // 2, tp % 2
    sibling_tp = chip * 2 + (1 - core)
    sibling = (me, sibling_tp)
    across = (me, (1 - chip) * 2 + core)

    def z_sibling(off):
        return (grp_of(x, (z + off) % 8, yh), sibling_tp)

    def remote(src, dst, send, recv, device):
        return pltpu.make_async_remote_copy(
            src_ref=src, dst_ref=dst, send_sem=send, recv_sem=recv,
            device_id=device, device_id_type=MESH,
        )

    barrier = pltpu.get_barrier_semaphore()
    for off in Z_FAR:
        pl.semaphore_signal(barrier, inc=1, device_id=z_peer(off)[1], device_id_type=MESH)
    for off in B_FAR:
        pl.semaphore_signal(barrier, inc=1, device_id=b_peer(off)[1], device_id_type=MESH)
    for off in Z_FAR:
        pl.semaphore_signal(barrier, inc=1, device_id=z_sibling(off), device_id_type=MESH)
    for device in (across, sibling):
        pl.semaphore_signal(barrier, inc=1, device_id=device, device_id_type=MESH)

    ints = [
        pltpu.make_async_copy(pre_hbm, pre_s, lint.at[0]),
        pltpu.make_async_copy(sam_hbm, sam_s, lint.at[1]),
        pltpu.make_async_copy(sam_hbm, sam_v, lint.at[2]),
        pltpu.make_async_copy(len_hbm, len_s, lint.at[3]),
    ]
    for copy in ints:
        copy.start()
    for i in range(HEADS):
        pltpu.make_async_copy(q_hbm.at[:, pl.ds(i * HD, HD)], qh.at[i], lq).start()
    for part in range(2):
        for k in range(KVHEADS):
            pltpu.make_async_copy(
                kv_hbm.at[0, part, :, pl.ds(k * HD, HD)], kv.at[part, k], lkv
            ).start()
    for part in range(2):
        for k in range(KVHEADS):
            pltpu.make_async_copy(
                suf_hbm.at[:, part, :, pl.ds(k * HD, HD)], suf.at[part, k], lsuf
            ).start()
    small = [
        pltpu.make_async_copy(gain_hbm, gain, lsmall.at[0]),
        pltpu.make_async_copy(res_hbm, res, lsmall.at[1]),
    ]
    for copy in small:
        copy.start()

    def quarter(q, of_core):
        return w_hbm.at[:, pl.ds(pl.multiple_of((2 * q + of_core) * COLS, HD), COLS)]

    for q in range(2):
        pltpu.make_async_copy(quarter(q, core), w.at[0, q], lw).start()

    for copy in ints:
        copy.wait()

    line = [z_peer(off)[1][0] for off in range(8)]

    def find(p, found):
        group = pre_s[p]
        return tuple(found[off] + jnp.where(group == line[off], p, 0) for off in range(8))

    found = lax.fori_loop(0, PROMPTS, find, (jnp.int32(0),) * 8)
    for off in range(8):
        own_p[off] = found[off]
        for s in range(SLOTS):
            pick_s[off * SLOTS + s] = sam_s[s, found[off] & 63]

    pltpu.make_async_copy(qh, qh, lq).wait()
    pl.semaphore_wait(barrier, 23)

    for off in Z_FAR:
        zz, device = z_peer(off)
        remote(qh.at[zz], qall.at[off], sa, ra.at[off], device).start()
    qall[0] = qh[z]

    for q in range(2):
        remote(quarter(q, 1 - core), w.at[1, q], sw, rw, sibling).start()

    for off in (0,) + Z_NEAR:
        block = qall.at[off]
        if off != 0:
            remote(qh.at[0], block, sa, ra.at[off], (me, tp)).wait_recv()
        for boff in B_FAR:
            slot = (boff[0] * 2 + boff[1]) * 8 + off
            remote(block, qall.at[slot], sb, rb, b_peer(boff)[1]).start()
    pltpu.make_async_copy(suf, suf, lsuf).wait()
    col = lax.broadcasted_iota(i32, (32, 512), 1)
    srow = lax.broadcasted_iota(i32, (32, 512), 0) & 15
    col_sample = col >> 5
    live_len = jnp.zeros((32, 512), i32)
    for s in range(SAMP):
        live_len = jnp.where(col_sample == s, len_s[s], live_len)
    live = (col_sample == srow) & ((col & 31) < live_len)
    lower = lax.broadcasted_iota(i32, (8, HD), 1) < 64
    for k in range(KVHEADS):
        query = qh[pl.ds(2 * k, 2)].reshape(32, HD)
        scores = (
            lax.dot_general(
                query, suf[0, k].reshape(512, HD), (((1,), (1,)), ((), ())),
                preferred_element_type=f32,
            )
            * SCORE_SCALE
        )
        top = jnp.max(jnp.where(live, scores, NEG), axis=1, keepdims=True)
        weights = jnp.where(live, jnp.exp(jnp.where(live, scores - top, 0.0)), 0.0)
        total = jnp.sum(weights, axis=1, keepdims=True)
        out = (
            jnp.dot(weights.astype(bf16), suf[1, k].reshape(512, HD), preferred_element_type=f32)
            / total
        )
        logs = jnp.broadcast_to(top + jnp.log(total), (32, HD))
        for h in range(2):
            at = h * SAMP
            sxs[2 * k + h, pl.ds(0, SAMP)] = out[at : at + SAMP]
            sxs[2 * k + h, pl.ds(SAMP, 8)] = jnp.where(
                lower, logs[at : at + 8], logs[at + 8 : at + 16]
            )
    for off in Z_FAR:
        zz, device = z_peer(off)
        remote(sxs.at[zz], sx.at[off], ssx, rsx, device).start()
    sx[0] = sxs[z]

    others = qall.at[pl.ds(8, 56)]
    remote(others, others, sb, rb, (me, tp)).wait_recv()

    for off in Z_FAR + (0,):
        for s in range(SLOTS):
            g = pick_s[off * SLOTS + s]
            slot = (((x - (g >> 4)) & 3) * 2 + ((yh - g) & 1)) * 8 + ((z - (g >> 1)) & 7)
            block = qall[slot]
            if off == 0:
                qc[0, pl.ds(s * SAMP, SAMP)] = block
            else:
                csend[off, pl.ds(s * SAMP, SAMP)] = block
        if off != 0:
            remote(csend.at[off], qc.at[off], sc, rcs.at[off], z_peer(off)[1]).start()

    lane = lax.broadcasted_iota(i32, (1, 512), 1)
    lane_block = lane >> 4
    lane_row = lane & 15
    group_lane = jnp.zeros((1, 512), i32)
    prompt_lane = jnp.zeros((1, 512), i32)
    for c in range(32):
        group_lane = jnp.where(lane_block == c, pick_s[c], group_lane)
    for off in range(8):
        prompt_lane = jnp.where((lane >> 6) == off, own_p[off], prompt_lane)
    pick_b = (((group_lane >> 4) - x) & 3) * 2 + ((group_lane - yh) & 1)
    pick_z = ((group_lane >> 1) - z) & 7
    table = jnp.transpose(sam_v[...])
    member = jnp.zeros((PROMPTS, 512), f32)
    for s in range(SLOTS):
        member = member + jnp.where(table[:, s : s + 1] == group_lane, 1.0, 0.0)
    prompt_row = lax.broadcasted_iota(i32, (PROMPTS, 512), 0)
    count = jnp.sum(member, axis=0, keepdims=True)
    rank = jnp.sum(jnp.where(prompt_row < prompt_lane, member, 0.0), axis=0, keepdims=True)
    row = lane_row.astype(f32)
    rest = row - jnp.floor((row + 0.5) / count) * count
    owned = rest == rank
    place = jnp.where(owned, (pick_b * 8 + pick_z) * SAMP + lane_row, -1)
    place2 = jnp.where(owned, pick_b * SAMP + lane_row, -1)
    few = lax.broadcasted_iota(i32, (SAMP, 512), 0)

    def one_hot(first, wanted):
        return jnp.where(few + first * SAMP == wanted, 1.0, 0.0).astype(bf16)

    for n in range(8):
        for at, off in enumerate(Z_FAR[:3]):
            hot1[n, pl.ds(at * SAMP, SAMP)] = one_hot(n * 8 + off, place)
        hot1[n, pl.ds(48, SAMP)] = one_hot(n, place2)
        for at, off in enumerate(Z_FAR[3:] + (0,)):
            hot2[n, pl.ds(at * SAMP, SAMP)] = one_hot(n * 8 + off, place)
    tile_lane = lax.broadcasted_iota(i32, (SAMP, HD), 1)
    for c in range(32):
        of_z = ((pick_s[c] >> 1) - z) & 7
        keep = ((tile_lane >> 3) == of_z) & (((tile_lane & 7) >> 1) == c % SLOTS)
        lmask[pl.ds(c * SAMP, SAMP)] = jnp.where(keep, 1.0, 0.0).astype(bf16)

    pltpu.make_async_copy(kv, kv, lkv).wait()

    def attend(off):
        k = z_peer(-off)[0] // 2
        scores = (
            lax.dot_general(
                qc[off], kv[0, k], (((1,), (1,)), ((), ())), preferred_element_type=f32
            )
            * SCORE_SCALE
        )
        top = jnp.max(scores, axis=1, keepdims=True)
        weights = jnp.exp(scores - top)
        total = jnp.sum(weights, axis=1, keepdims=True)
        out = jnp.dot(weights.astype(bf16), kv[1, k], preferred_element_type=f32) / total
        log_total = top + jnp.log(total)
        high = log_total.astype(bf16).astype(f32)
        low = log_total - high
        tile = jnp.zeros((SAMP, HD), f32)
        for s in range(SLOTS):
            at = s * SAMP
            tile = jnp.where((tile_lane & 7) == 2 * s, high[at : at + SAMP], tile)
            tile = jnp.where((tile_lane & 7) == 2 * s + 1, low[at : at + SAMP], tile)
        return out.astype(bf16), tile.astype(bf16)

    for group in ((4,), (3, 5), (2, 6), (1, 7), (0,)):
        for off in group:
            if off != 0:
                remote(csend.at[off], qc.at[off], sc, rcs.at[off], (me, tp)).wait_recv()
        results = [attend(off) for off in group]
        for off, (out, tile) in zip(group, results):
            result = rc if off == 0 else rsend
            result[off, pl.ds(0, 64)] = out
            result[off, pl.ds(64, SAMP)] = tile
            if off != 0:
                remote(
                    rsend.at[off], rc.at[off], sct, rct, z_peer(-off)[1]
                ).start()

    seven = rc.at[pl.ds(1, 7)]
    remote(seven, seven, sct, rct, (me, tp)).wait_recv()
    results = rc[:, pl.ds(0, 64)].reshape(512, HD)
    logs = jnp.concatenate(
        [rc[off, pl.ds(64, SAMP)] for off in range(8) for _ in range(SLOTS)], axis=0
    ) * lmask[...]
    both = jnp.concatenate([results, logs], axis=1)

    def from_b(boff):
        n = boff[0] * 2 + boff[1]
        first, second = (bt1, bt2) if n == 0 else (bsend1, bsend2)
        return n, first.at[n], second.at[n]

    for boff in B_FAR + ((0, 0),):
        n, first, _ = from_b(boff)
        picked = jnp.dot(hot1[n], both, preferred_element_type=f32).astype(bf16)
        first[pl.ds(0, 48)] = picked[:48, :HD]
        first[pl.ds(48, SAMP)] = picked[48:, HD:]
        if n != 0:
            remote(first, bt1.at[n], sbt.at[0], rbt.at[0], b_peer(boff)[1]).start()
    for boff in B_FAR + ((0, 0),):
        n, _, second = from_b(boff)
        second[...] = jnp.dot(hot2[n], results, preferred_element_type=f32).astype(bf16)
        if n != 0:
            remote(second, bt2.at[n], sbt.at[1], rbt.at[1], b_peer(boff)[1]).start()

    def merge(ref):
        merged = ref[0].astype(f32)
        for n in range(1, 8):
            merged = merged + ref[n].astype(f32)
        return merged

    def give(off, prefix_out):
        prefix_log = jnp.sum(
            jnp.where((tile_lane >> 3) == off, logs, 0.0), axis=1, keepdims=True
        )
        suffix = sx[(8 - off) % 8]
        suffix_log = jnp.concatenate([suffix[SAMP:, :1], suffix[SAMP:, 64:65]], axis=0)
        joint = jnp.maximum(prefix_log, suffix_log)
        share_p = jnp.exp(prefix_log - joint)
        share_s = jnp.exp(suffix_log - joint)
        attended = (share_p * prefix_out + share_s * suffix[:SAMP]) / (share_p + share_s)
        asend[off] = attended.astype(bf16)
        if off == 0:
            fin[0] = asend[0]
            remote(asend.at[0], fin.at[8], sat, rat, sibling).start()
        else:
            remote(asend.at[off], fin.at[off], sat, rat, z_peer(off)[1]).start()
            remote(asend.at[off], fin.at[8 + off], sat, rat, z_sibling(off)).start()

    seven = sx.at[pl.ds(1, 7)]
    remote(seven, seven, ssx, rsx, (me, tp)).wait_recv()
    seven = bt1.at[pl.ds(1, 7)]
    remote(seven, seven, sbt.at[0], rbt.at[0], (me, tp)).wait_recv()
    merged = merge(bt1)
    logs = merged[48:]
    for at, off in enumerate(Z_FAR[:3]):
        give(off, merged[at * SAMP : (at + 1) * SAMP])
    seven = bt2.at[pl.ds(1, 7)]
    remote(seven, seven, sbt.at[1], rbt.at[1], (me, tp)).wait_recv()
    merged = merge(bt2)
    for at, off in enumerate(Z_FAR[3:] + (0,)):
        give(off, merged[at * SAMP : (at + 1) * SAMP])
    pltpu.make_async_copy(w.at[0], w.at[0], lw).wait()
    remote(w.at[0], w.at[1], sw, rw, sibling).wait_recv()
    others = fin.at[pl.ds(0, 15)]
    remote(others, others, sat, rat, (me, tp)).wait_recv()

    attended = [
        jnp.concatenate([fin[side * 8 + (z - i) % 8] for i in range(HEADS)], axis=1)
        for side in range(2)
    ]

    def project(q):
        return sum(
            jnp.dot(attended[side], w[side, q], preferred_element_type=f32)
            for side in range(2)
        )

    other_part = project(1 - chip)
    psend[0] = other_part.astype(bf16)
    remote(psend.at[0], pr.at[0], srs, rrs, across).start()
    own_part = project(chip)
    psend[1] = own_part.astype(bf16)
    remote(psend.at[1], pr.at[1], srs, rrs, across).start()
    for copy in small:
        copy.wait()
    remote(psend, pr, srs, rrs, across).wait_recv()
    projected = own_part + pr[0].astype(f32)
    twin = other_part + pr[1].astype(f32)
    squares = jnp.zeros((SAMP, HD), f32)
    for n in range(COLS // HD):
        for whole in (projected, twin):
            piece = whole[:, n * HD : (n + 1) * HD]
            squares = squares + piece * piece
    sqs[...] = squares
    remote(sqs, sqr, ssq, rsq, sibling).start()
    remote(sqs, sqr, ssq, rsq, sibling).wait_recv()
    squares = squares + sqr[...]
    scale = lax.rsqrt(jnp.sum(squares, axis=1, keepdims=True) / D + NORM_EPS)
    o_ref[...] = (res[...].astype(f32) + projected * scale * gain[...].reshape(1, COLS)).astype(bf16)

    for ref, count, send, recv in (
        (qall, 7, sa, ra.at[0]), (qall, 56, sb, rb), (csend, 7, sc, rcs.at[0]),
        (rc, 7, sct, rct), (bt1, 7, sbt.at[0], rbt.at[0]), (bt2, 7, sbt.at[1], rbt.at[1]),
        (sx, 7, ssx, rsx), (fin, 15, sat, rat),
    ):
        some = ref.at[pl.ds(0, count)]
        remote(some, some, send, recv, (me, tp)).wait_send()
    remote(w.at[0], w.at[1], sw, rw, sibling).wait_send()
    remote(psend, pr, srs, rrs, across).wait_send()
    remote(sqs, sqr, ssq, rsq, sibling).wait_send()


def shards(
    queries, prefix_kv, suffix_kv, suffix_len, prefill_group, sampler_groups,
    out_weight, norm_gain, residual,
):
    vmem = pltpu.VMEM
    dma = pltpu.SemaphoreType.DMA
    scratch = [
        vmem((HEADS, SAMP, HD), bf16),
        vmem((2, KVHEADS, PREFIX, HD), bf16),
        vmem((2, KVHEADS, SAMP, SUF, HD), bf16),
        vmem((2, 2, HEADS * HD, COLS), bf16),
        vmem((COLS,), f32),
        vmem((SAMP, COLS), bf16),
        pltpu.SMEM((SAMP,), i32),
        pltpu.SMEM((PROMPTS,), i32),
        pltpu.SMEM((SLOTS, PROMPTS), i32),
        vmem((SLOTS, PROMPTS), i32),
        pltpu.SMEM((8,), i32),
        pltpu.SMEM((32,), i32),
        vmem((64, SAMP, HD), bf16),
        vmem((8, 64, HD), bf16),
        vmem((8, 64, HD), bf16),
        vmem((8, 80, HD), bf16),
        vmem((8, 80, HD), bf16),
        vmem((8, 64, HD), bf16),
        vmem((8, 80, HD), bf16),
        vmem((8, 64, HD), bf16),
        vmem((8, 80, HD), bf16),
        vmem((8, SAMP, HD), bf16),
        vmem((16, SAMP, HD), bf16),
        vmem((8, 64, 512), bf16),
        vmem((8, 80, 512), bf16),
        vmem((512, HD), bf16),
        vmem((8, 24, HD), f32),
        vmem((8, 24, HD), f32),
        vmem((2, SAMP, COLS), bf16),
        vmem((2, SAMP, COLS), bf16),
        vmem((SAMP, HD), f32),
        vmem((SAMP, HD), f32),
        dma, dma, dma, dma, dma((2,)), dma((4,)),
        dma, dma((8,)),
        dma, dma,
        dma, dma((8,)),
        dma, dma,
        dma((2,)), dma((2,)),
        dma, dma,
        dma, dma,
        dma, dma,
        dma, dma,
        dma, dma,
    ]
    anywhere = pl.BlockSpec(memory_space=pl.ANY)
    return pl.pallas_call(
        kernel,
        out_shape=jax.ShapeDtypeStruct(residual.shape, bf16),
        in_specs=[anywhere] * 9,
        out_specs=pl.BlockSpec(memory_space=pltpu.VMEM),
        scratch_shapes=scratch,
        compiler_params=pltpu.CompilerParams(
            collective_id=0, has_side_effects=True, vmem_limit_bytes=63 * 1024 * 1024
        ),
        cost_estimate=pl.CostEstimate(
            flops=500_000_000, bytes_accessed=13_000_000, transcendentals=600_000
        ),
    )(
        queries, prefix_kv, suffix_kv, suffix_len, prefill_group, sampler_groups.T,
        out_weight, norm_gain, residual,
    )


def solution(mesh):
    in_specs = (
        P("grp", "tp"),
        P("grp", None, None, "tp"),
        P("grp", None, None, "tp"),
        P("grp"),
        P(),
        P(),
        P("tp", None),
        P("tp"),
        P("grp", "tp"),
    )
    return jax.shard_map(
        shards, mesh=mesh, in_specs=in_specs, out_specs=P("grp", "tp"), check_vma=False
    )
```

```python
import jax
import jax.numpy as jnp
from jax import lax
from jax.experimental import pallas as pl
from jax.experimental.pallas import tpu as pltpu
from jax.sharding import PartitionSpec as P

MESH = pl.DeviceIdType.MESH
D = 4608
HD = 128
SAMP = 16
SLOTS = 4
PREFIX = 1024
SUF = 32
HEADS = 8
KVHEADS = 4
COLS = 1152
PROMPTS = 64
SCORE_SCALE = 144.0 ** (-0.5)
NORM_EPS = 1e-06
NEG = -1e30

Z_FAR = (4, 3, 5, 2, 6, 1, 7)
Z_NEAR = (1, 7, 2, 6, 3, 5, 4)
B_FAR = ((2, 1), (1, 1), (3, 1), (2, 0), (0, 1), (1, 0), (3, 0))

f32 = jnp.float32
bf16 = jnp.bfloat16
i32 = jnp.int32


def kernel(
    q_hbm, kv_hbm, suf_hbm, len_hbm, pre_hbm, sam_hbm, w_hbm, gain_hbm, res_hbm,
    o_ref,
    qh, kv, suf, w, gain, res, len_s, pre_s, sam_s, sam_v,
    own_p, pick_s,
    qall, csend, qc, rsend, rc, bsend1, bsend2, bt1, bt2, asend, fin,
    hot1, hot2, lmask, sxs, sx, psend, pr, sqs, sqr,
    lq, lkv, lsuf, lw, lsmall, lint,
    sa, ra, sb, rb, sc, rcs, sct, rct, sbt, rbt, sat, rat, srs, rrs, ssq, rsq, sw, rw, ssx, rsx,
):
    me = lax.axis_index("grp")
    tp = lax.axis_index("tp")
    x = me // 16
    z = (me // 2) % 8
    yh = me % 2
    b = x * 2 + yh

    def grp_of(xx, zz, yy):
        return (xx * 8 + zz) * 2 + yy

    def z_peer(off):
        zz = (z + off) % 8
        return zz, (grp_of(x, zz, yh), tp)

    def b_peer(off):
        xx = (x + off[0]) % 4
        yy = (yh + off[1]) % 2
        return xx * 2 + yy, (grp_of(xx, z, yy), tp)

    chip, core = tp // 2, tp % 2
    sibling_tp = chip * 2 + (1 - core)
    sibling = (me, sibling_tp)
    across = (me, (1 - chip) * 2 + core)

    def z_sibling(off):
        return (grp_of(x, (z + off) % 8, yh), sibling_tp)

    def remote(src, dst, send, recv, device):
        return pltpu.make_async_remote_copy(
            src_ref=src, dst_ref=dst, send_sem=send, recv_sem=recv,
            device_id=device, device_id_type=MESH,
        )

    barrier = pltpu.get_barrier_semaphore()
    for off in Z_FAR:
        pl.semaphore_signal(barrier, inc=1, device_id=z_peer(off)[1], device_id_type=MESH)
    for off in B_FAR:
        pl.semaphore_signal(barrier, inc=1, device_id=b_peer(off)[1], device_id_type=MESH)
    for off in Z_FAR:
        pl.semaphore_signal(barrier, inc=1, device_id=z_sibling(off), device_id_type=MESH)
    for device in (across, sibling):
        pl.semaphore_signal(barrier, inc=1, device_id=device, device_id_type=MESH)

    ints = [
        pltpu.make_async_copy(pre_hbm, pre_s, lint.at[0]),
        pltpu.make_async_copy(sam_hbm, sam_s, lint.at[1]),
        pltpu.make_async_copy(sam_hbm, sam_v, lint.at[2]),
        pltpu.make_async_copy(len_hbm, len_s, lint.at[3]),
    ]
    for copy in ints:
        copy.start()
    for i in range(HEADS):
        pltpu.make_async_copy(q_hbm.at[:, pl.ds(i * HD, HD)], qh.at[i], lq).start()
    for part in range(2):
        for k in range(KVHEADS):
            pltpu.make_async_copy(
                kv_hbm.at[0, part, :, pl.ds(k * HD, HD)], kv.at[part, k], lkv
            ).start()
    for part in range(2):
        for k in range(KVHEADS):
            pltpu.make_async_copy(
                suf_hbm.at[:, part, :, pl.ds(k * HD, HD)], suf.at[part, k], lsuf
            ).start()
    small = [
        pltpu.make_async_copy(gain_hbm, gain, lsmall.at[0]),
        pltpu.make_async_copy(res_hbm, res, lsmall.at[1]),
    ]
    for copy in small:
        copy.start()

    def quarter(q, of_core):
        return w_hbm.at[:, pl.ds(pl.multiple_of((2 * q + of_core) * COLS, HD), COLS)]

    for q in range(2):
        pltpu.make_async_copy(quarter(q, core), w.at[0, q], lw).start()

    for copy in ints:
        copy.wait()

    line = [z_peer(off)[1][0] for off in range(8)]

    def find(p, found):
        group = pre_s[p]
        return tuple(found[off] + jnp.where(group == line[off], p, 0) for off in range(8))

    found = lax.fori_loop(0, PROMPTS, find, (jnp.int32(0),) * 8)
    for off in range(8):
        own_p[off] = found[off]
        for s in range(SLOTS):
            pick_s[off * SLOTS + s] = sam_s[s, found[off] & 63]

    pltpu.make_async_copy(qh, qh, lq).wait()
    pl.semaphore_wait(barrier, 23)

    for off in Z_FAR:
        zz, device = z_peer(off)
        remote(qh.at[zz], qall.at[off], sa, ra.at[off], device).start()
    qall[0] = qh[z]

    for q in range(2):
        remote(quarter(q, 1 - core), w.at[1, q], sw, rw, sibling).start()

    for off in (0,) + Z_NEAR:
        block = qall.at[off]
        if off != 0:
            remote(qh.at[0], block, sa, ra.at[off], (me, tp)).wait_recv()
        for boff in B_FAR:
            slot = (boff[0] * 2 + boff[1]) * 8 + off
            remote(block, qall.at[slot], sb, rb, b_peer(boff)[1]).start()
    pltpu.make_async_copy(suf, suf, lsuf).wait()
    col = lax.broadcasted_iota(i32, (32, 512), 1)
    srow = lax.broadcasted_iota(i32, (32, 512), 0) & 15
    col_sample = col >> 5
    live_len = jnp.zeros((32, 512), i32)
    for s in range(SAMP):
        live_len = jnp.where(col_sample == s, len_s[s], live_len)
    live = (col_sample == srow) & ((col & 31) < live_len)
    lower = lax.broadcasted_iota(i32, (8, HD), 1) < 64
    for k in range(KVHEADS):
        query = qh[pl.ds(2 * k, 2)].reshape(32, HD)
        scores = (
            lax.dot_general(
                query, suf[0, k].reshape(512, HD), (((1,), (1,)), ((), ())),
                preferred_element_type=f32,
            )
            * SCORE_SCALE
        )
        top = jnp.max(jnp.where(live, scores, NEG), axis=1, keepdims=True)
        weights = jnp.where(live, jnp.exp(jnp.where(live, scores - top, 0.0)), 0.0)
        total = jnp.sum(weights, axis=1, keepdims=True)
        out = (
            jnp.dot(weights.astype(bf16), suf[1, k].reshape(512, HD), preferred_element_type=f32)
            / total
        )
        logs = jnp.broadcast_to(top + jnp.log(total), (32, HD))
        for h in range(2):
            at = h * SAMP
            sxs[2 * k + h, pl.ds(0, SAMP)] = out[at : at + SAMP]
            sxs[2 * k + h, pl.ds(SAMP, 8)] = jnp.where(
                lower, logs[at : at + 8], logs[at + 8 : at + 16]
            )
    for off in Z_FAR:
        zz, device = z_peer(off)
        remote(sxs.at[zz], sx.at[off], ssx, rsx, device).start()
    sx[0] = sxs[z]

    others = qall.at[pl.ds(8, 56)]
    remote(others, others, sb, rb, (me, tp)).wait_recv()

    for off in Z_FAR + (0,):
        for s in range(SLOTS):
            g = pick_s[off * SLOTS + s]
            slot = (((x - (g >> 4)) & 3) * 2 + ((yh - g) & 1)) * 8 + ((z - (g >> 1)) & 7)
            block = qall[slot]
            if off == 0:
                qc[0, pl.ds(s * SAMP, SAMP)] = block
            else:
                csend[off, pl.ds(s * SAMP, SAMP)] = block
        if off != 0:
            remote(csend.at[off], qc.at[off], sc, rcs.at[off], z_peer(off)[1]).start()

    lane = lax.broadcasted_iota(i32, (1, 512), 1)
    lane_block = lane >> 4
    lane_row = lane & 15
    group_lane = jnp.zeros((1, 512), i32)
    prompt_lane = jnp.zeros((1, 512), i32)
    for c in range(32):
        group_lane = jnp.where(lane_block == c, pick_s[c], group_lane)
    for off in range(8):
        prompt_lane = jnp.where((lane >> 6) == off, own_p[off], prompt_lane)
    pick_b = (((group_lane >> 4) - x) & 3) * 2 + ((group_lane - yh) & 1)
    pick_z = ((group_lane >> 1) - z) & 7
    table = jnp.transpose(sam_v[...])
    member = jnp.zeros((PROMPTS, 512), f32)
    for s in range(SLOTS):
        member = member + jnp.where(table[:, s : s + 1] == group_lane, 1.0, 0.0)
    prompt_row = lax.broadcasted_iota(i32, (PROMPTS, 512), 0)
    count = jnp.sum(member, axis=0, keepdims=True)
    rank = jnp.sum(jnp.where(prompt_row < prompt_lane, member, 0.0), axis=0, keepdims=True)
    row = lane_row.astype(f32)
    rest = row - jnp.floor((row + 0.5) / count) * count
    owned = rest == rank
    place = jnp.where(owned, (pick_b * 8 + pick_z) * SAMP + lane_row, -1)
    place2 = jnp.where(owned, pick_b * SAMP + lane_row, -1)
    few = lax.broadcasted_iota(i32, (SAMP, 512), 0)

    def one_hot(first, wanted):
        return jnp.where(few + first * SAMP == wanted, 1.0, 0.0).astype(bf16)

    for n in range(8):
        for at, off in enumerate(Z_FAR[:3]):
            hot1[n, pl.ds(at * SAMP, SAMP)] = one_hot(n * 8 + off, place)
        hot1[n, pl.ds(48, SAMP)] = one_hot(n, place2)
        for at, off in enumerate(Z_FAR[3:] + (0,)):
            hot2[n, pl.ds(at * SAMP, SAMP)] = one_hot(n * 8 + off, place)
    tile_lane = lax.broadcasted_iota(i32, (SAMP, HD), 1)
    for c in range(32):
        of_z = ((pick_s[c] >> 1) - z) & 7
        keep = ((tile_lane >> 3) == of_z) & (((tile_lane & 7) >> 1) == c % SLOTS)
        lmask[pl.ds(c * SAMP, SAMP)] = jnp.where(keep, 1.0, 0.0).astype(bf16)

    pltpu.make_async_copy(kv, kv, lkv).wait()

    def attend(off):
        k = z_peer(-off)[0] // 2
        scores = (
            lax.dot_general(
                qc[off], kv[0, k], (((1,), (1,)), ((), ())), preferred_element_type=f32
            )
            * SCORE_SCALE
        )
        top = jnp.max(scores, axis=1, keepdims=True)
        weights = jnp.exp(scores - top)
        total = jnp.sum(weights, axis=1, keepdims=True)
        out = jnp.dot(weights.astype(bf16), kv[1, k], preferred_element_type=f32) / total
        log_total = top + jnp.log(total)
        high = log_total.astype(bf16).astype(f32)
        low = log_total - high
        tile = jnp.zeros((SAMP, HD), f32)
        for s in range(SLOTS):
            at = s * SAMP
            tile = jnp.where((tile_lane & 7) == 2 * s, high[at : at + SAMP], tile)
            tile = jnp.where((tile_lane & 7) == 2 * s + 1, low[at : at + SAMP], tile)
        return out.astype(bf16), tile.astype(bf16)

    for group in ((4,), (3, 5), (2, 6), (1, 7), (0,)):
        for off in group:
            if off != 0:
                remote(csend.at[off], qc.at[off], sc, rcs.at[off], (me, tp)).wait_recv()
        results = [attend(off) for off in group]
        for off, (out, tile) in zip(group, results):
            result = rc if off == 0 else rsend
            result[off, pl.ds(0, 64)] = out
            result[off, pl.ds(64, SAMP)] = tile
            if off != 0:
                remote(
                    rsend.at[off], rc.at[off], sct, rct, z_peer(-off)[1]
                ).start()

    seven = rc.at[pl.ds(1, 7)]
    remote(seven, seven, sct, rct, (me, tp)).wait_recv()
    results = rc[:, pl.ds(0, 64)].reshape(512, HD)
    logs = jnp.concatenate(
        [rc[off, pl.ds(64, SAMP)] for off in range(8) for _ in range(SLOTS)], axis=0
    ) * lmask[...]
    both = jnp.concatenate([results, logs], axis=1)

    def from_b(boff):
        n = boff[0] * 2 + boff[1]
        first, second = (bt1, bt2) if n == 0 else (bsend1, bsend2)
        return n, first.at[n], second.at[n]

    for boff in B_FAR + ((0, 0),):
        n, first, _ = from_b(boff)
        picked = jnp.dot(hot1[n], both, preferred_element_type=f32).astype(bf16)
        first[pl.ds(0, 48)] = picked[:48, :HD]
        first[pl.ds(48, SAMP)] = picked[48:, HD:]
        if n != 0:
            remote(first, bt1.at[n], sbt.at[0], rbt.at[0], b_peer(boff)[1]).start()
    for boff in B_FAR + ((0, 0),):
        n, _, second = from_b(boff)
        second[...] = jnp.dot(hot2[n], results, preferred_element_type=f32).astype(bf16)
        if n != 0:
            remote(second, bt2.at[n], sbt.at[1], rbt.at[1], b_peer(boff)[1]).start()

    def merge(ref):
        merged = ref[0].astype(f32)
        for n in range(1, 8):
            merged = merged + ref[n].astype(f32)
        return merged

    def give(off, prefix_out):
        prefix_log = jnp.sum(
            jnp.where((tile_lane >> 3) == off, logs, 0.0), axis=1, keepdims=True
        )
        suffix = sx[(8 - off) % 8]
        suffix_log = jnp.concatenate([suffix[SAMP:, :1], suffix[SAMP:, 64:65]], axis=0)
        joint = jnp.maximum(prefix_log, suffix_log)
        share_p = jnp.exp(prefix_log - joint)
        share_s = jnp.exp(suffix_log - joint)
        attended = (share_p * prefix_out + share_s * suffix[:SAMP]) / (share_p + share_s)
        asend[off] = attended.astype(bf16)
        if off == 0:
            fin[0] = asend[0]
            remote(asend.at[0], fin.at[8], sat, rat, sibling).start()
        else:
            remote(asend.at[off], fin.at[off], sat, rat, z_peer(off)[1]).start()
            remote(asend.at[off], fin.at[8 + off], sat, rat, z_sibling(off)).start()

    seven = sx.at[pl.ds(1, 7)]
    remote(seven, seven, ssx, rsx, (me, tp)).wait_recv()
    seven = bt1.at[pl.ds(1, 7)]
    remote(seven, seven, sbt.at[0], rbt.at[0], (me, tp)).wait_recv()
    merged = merge(bt1)
    logs = merged[48:]
    for at, off in enumerate(Z_FAR[:3]):
        give(off, merged[at * SAMP : (at + 1) * SAMP])
    seven = bt2.at[pl.ds(1, 7)]
    remote(seven, seven, sbt.at[1], rbt.at[1], (me, tp)).wait_recv()
    merged = merge(bt2)
    for at, off in enumerate(Z_FAR[3:] + (0,)):
        give(off, merged[at * SAMP : (at + 1) * SAMP])
    pltpu.make_async_copy(w.at[0], w.at[0], lw).wait()
    remote(w.at[0], w.at[1], sw, rw, sibling).wait_recv()
    others = fin.at[pl.ds(0, 15)]
    remote(others, others, sat, rat, (me, tp)).wait_recv()

    attended = [
        jnp.concatenate([fin[side * 8 + (z - i) % 8] for i in range(HEADS)], axis=1)
        for side in range(2)
    ]

    def project(q, slot):
        parts = []
        for start, stop in ((0, 512), (512, COLS)):
            at = pl.ds(start, stop - start)
            part = sum(
                jnp.dot(attended[side], w[side, q, :, at], preferred_element_type=f32)
                for side in range(2)
            )
            psend[slot, :, at] = part.astype(bf16)
            remote(psend.at[slot, :, at], pr.at[slot, :, at], srs, rrs, across).start()
            parts.append(part)
        return jnp.concatenate(parts, axis=1)

    other_part = project(1 - chip, 0)
    own_part = project(chip, 1)
    for copy in small:
        copy.wait()
    remote(psend, pr, srs, rrs, across).wait_recv()
    projected = own_part + pr[0].astype(f32)
    twin = other_part + pr[1].astype(f32)
    squares = jnp.zeros((SAMP, HD), f32)
    for n in range(COLS // HD):
        for whole in (projected, twin):
            piece = whole[:, n * HD : (n + 1) * HD]
            squares = squares + piece * piece
    sqs[...] = squares
    remote(sqs, sqr, ssq, rsq, sibling).start()
    remote(sqs, sqr, ssq, rsq, sibling).wait_recv()
    squares = squares + sqr[...]
    scale = lax.rsqrt(jnp.sum(squares, axis=1, keepdims=True) / D + NORM_EPS)
    o_ref[...] = (res[...].astype(f32) + projected * scale * gain[...].reshape(1, COLS)).astype(bf16)

    for ref, count, send, recv in (
        (qall, 7, sa, ra.at[0]), (qall, 56, sb, rb), (csend, 7, sc, rcs.at[0]),
        (rc, 7, sct, rct), (bt1, 7, sbt.at[0], rbt.at[0]), (bt2, 7, sbt.at[1], rbt.at[1]),
        (sx, 7, ssx, rsx), (fin, 15, sat, rat),
    ):
        some = ref.at[pl.ds(0, count)]
        remote(some, some, send, recv, (me, tp)).wait_send()
    remote(w.at[0], w.at[1], sw, rw, sibling).wait_send()
    remote(psend, pr, srs, rrs, across).wait_send()
    remote(sqs, sqr, ssq, rsq, sibling).wait_send()


def shards(
    queries, prefix_kv, suffix_kv, suffix_len, prefill_group, sampler_groups,
    out_weight, norm_gain, residual,
):
    vmem = pltpu.VMEM
    dma = pltpu.SemaphoreType.DMA
    scratch = [
        vmem((HEADS, SAMP, HD), bf16),
        vmem((2, KVHEADS, PREFIX, HD), bf16),
        vmem((2, KVHEADS, SAMP, SUF, HD), bf16),
        vmem((2, 2, HEADS * HD, COLS), bf16),
        vmem((COLS,), f32),
        vmem((SAMP, COLS), bf16),
        pltpu.SMEM((SAMP,), i32),
        pltpu.SMEM((PROMPTS,), i32),
        pltpu.SMEM((SLOTS, PROMPTS), i32),
        vmem((SLOTS, PROMPTS), i32),
        pltpu.SMEM((8,), i32),
        pltpu.SMEM((32,), i32),
        vmem((64, SAMP, HD), bf16),
        vmem((8, 64, HD), bf16),
        vmem((8, 64, HD), bf16),
        vmem((8, 80, HD), bf16),
        vmem((8, 80, HD), bf16),
        vmem((8, 64, HD), bf16),
        vmem((8, 80, HD), bf16),
        vmem((8, 64, HD), bf16),
        vmem((8, 80, HD), bf16),
        vmem((8, SAMP, HD), bf16),
        vmem((16, SAMP, HD), bf16),
        vmem((8, 64, 512), bf16),
        vmem((8, 80, 512), bf16),
        vmem((512, HD), bf16),
        vmem((8, 24, HD), f32),
        vmem((8, 24, HD), f32),
        vmem((2, SAMP, COLS), bf16),
        vmem((2, SAMP, COLS), bf16),
        vmem((SAMP, HD), f32),
        vmem((SAMP, HD), f32),
        dma, dma, dma, dma, dma((2,)), dma((4,)),
        dma, dma((8,)),
        dma, dma,
        dma, dma((8,)),
        dma, dma,
        dma((2,)), dma((2,)),
        dma, dma,
        dma, dma,
        dma, dma,
        dma, dma,
        dma, dma,
    ]
    anywhere = pl.BlockSpec(memory_space=pl.ANY)
    return pl.pallas_call(
        kernel,
        out_shape=jax.ShapeDtypeStruct(residual.shape, bf16),
        in_specs=[anywhere] * 9,
        out_specs=pl.BlockSpec(memory_space=pltpu.VMEM),
        scratch_shapes=scratch,
        compiler_params=pltpu.CompilerParams(
            collective_id=0, has_side_effects=True, vmem_limit_bytes=48 * 1024 * 1024
        ),
        cost_estimate=pl.CostEstimate(
            flops=500_000_000, bytes_accessed=13_000_000, transcendentals=600_000
        ),
    )(
        *[
            pltpu.with_memory_space_constraint(operand, pltpu.HBM)
            for operand in (
                queries, prefix_kv, suffix_kv, suffix_len, prefill_group, sampler_groups.T,
                out_weight, norm_gain, residual,
            )
        ]
    )


def solution(mesh):
    in_specs = (
        P("grp", "tp"),
        P("grp", None, None, "tp"),
        P("grp", None, None, "tp"),
        P("grp"),
        P(),
        P(),
        P("tp", None),
        P("tp"),
        P("grp", "tp"),
    )
    return jax.shard_map(
        shards, mesh=mesh, in_specs=in_specs, out_specs=P("grp", "tp"), check_vma=False
    )
```

```python
import jax
import jax.numpy as jnp
from jax import lax
from jax.experimental import pallas as pl
from jax.experimental.pallas import tpu as pltpu
from jax.sharding import PartitionSpec as P

MESH = pl.DeviceIdType.MESH
D = 4608
HD = 128
SAMP = 16
SLOTS = 4
PREFIX = 1024
SUF = 32
HEADS = 8
KVHEADS = 4
COLS = 1152
PROMPTS = 64
SCORE_SCALE = 144.0 ** (-0.5)
NORM_EPS = 1e-06
NEG = -1e30

Z_FAR = (4, 3, 5, 2, 6, 1, 7)
Z_NEAR = (1, 7, 2, 6, 3, 5, 4)
B_FAR = ((2, 1), (1, 1), (3, 1), (2, 0), (0, 1), (1, 0), (3, 0))

f32 = jnp.float32
bf16 = jnp.bfloat16
i32 = jnp.int32


def kernel(
    q_hbm, kv_hbm, suf_hbm, len_hbm, pre_hbm, sam_hbm, w_hbm, gain_hbm, res_hbm,
    o_ref,
    qh, kv, suf, w, gain, res, len_s, pre_s, sam_s, sam_v,
    own_p, pick_s, slot_s,
    qall, csend, qc, rsend, rc, bsend1, bsend2, bt1, bt2, asend, fin,
    hot1, hot2, lmask, sxs, sx, psend, pr, sqs, sqr,
    lq, lkv, lsuf, lw, lsmall, lint,
    sa, ra, sb, rb, sc, rcs, sct, rct, sbt, rbt, sat, rat, srs, rrs, ssq, rsq, sw, rw, ssx, rsx,
):
    me = lax.axis_index("grp")
    tp = lax.axis_index("tp")
    x = me // 16
    z = (me // 2) % 8
    yh = me % 2
    b = x * 2 + yh

    def grp_of(xx, zz, yy):
        return (xx * 8 + zz) * 2 + yy

    def z_peer(off):
        zz = (z + off) % 8
        return zz, (grp_of(x, zz, yh), tp)

    def b_peer(off):
        xx = (x + off[0]) % 4
        yy = (yh + off[1]) % 2
        return xx * 2 + yy, (grp_of(xx, z, yy), tp)

    chip, core = tp // 2, tp % 2
    sibling_tp = chip * 2 + (1 - core)
    sibling = (me, sibling_tp)
    across = (me, (1 - chip) * 2 + core)

    def z_sibling(off):
        return (grp_of(x, (z + off) % 8, yh), sibling_tp)

    def remote(src, dst, send, recv, device):
        return pltpu.make_async_remote_copy(
            src_ref=src, dst_ref=dst, send_sem=send, recv_sem=recv,
            device_id=device, device_id_type=MESH,
        )

    barrier = pltpu.get_barrier_semaphore()
    for off in Z_FAR:
        pl.semaphore_signal(barrier, inc=1, device_id=z_peer(off)[1], device_id_type=MESH)
    for off in B_FAR:
        pl.semaphore_signal(barrier, inc=1, device_id=b_peer(off)[1], device_id_type=MESH)
    for off in Z_FAR:
        pl.semaphore_signal(barrier, inc=1, device_id=z_sibling(off), device_id_type=MESH)
    for device in (across, sibling):
        pl.semaphore_signal(barrier, inc=1, device_id=device, device_id_type=MESH)

    ints = [
        pltpu.make_async_copy(pre_hbm, pre_s, lint.at[0]),
        pltpu.make_async_copy(sam_hbm, sam_s, lint.at[1]),
        pltpu.make_async_copy(sam_hbm, sam_v, lint.at[2]),
        pltpu.make_async_copy(len_hbm, len_s, lint.at[3]),
    ]
    for copy in ints:
        copy.start()
    for i in range(HEADS):
        pltpu.make_async_copy(q_hbm.at[:, pl.ds(i * HD, HD)], qh.at[i], lq).start()
    for part in range(2):
        for k in range(KVHEADS):
            pltpu.make_async_copy(
                kv_hbm.at[0, part, :, pl.ds(k * HD, HD)], kv.at[part, k], lkv
            ).start()
    for part in range(2):
        for k in range(KVHEADS):
            pltpu.make_async_copy(
                suf_hbm.at[:, part, :, pl.ds(k * HD, HD)], suf.at[part, k], lsuf
            ).start()
    small = [
        pltpu.make_async_copy(gain_hbm, gain, lsmall.at[0]),
        pltpu.make_async_copy(res_hbm, res, lsmall.at[1]),
    ]
    for copy in small:
        copy.start()

    def quarter(q, of_core):
        return w_hbm.at[:, pl.ds(pl.multiple_of((2 * q + of_core) * COLS, HD), COLS)]

    for q in range(2):
        pltpu.make_async_copy(quarter(q, core), w.at[0, q], lw).start()

    for copy in ints:
        copy.wait()

    line = [z_peer(off)[1][0] for off in range(8)]

    def find(p, found):
        group = pre_s[p]
        return tuple(found[off] + jnp.where(group == line[off], p, 0) for off in range(8))

    found = lax.fori_loop(0, PROMPTS, find, (jnp.int32(0),) * 8)
    for off in range(8):
        own_p[off] = found[off]
        for s in range(SLOTS):
            g = sam_s[s, found[off] & 63]
            pick_s[off * SLOTS + s] = g
            near = ((x - (g >> 4)) & 3) * 2 + ((yh - g) & 1)
            slot_s[off * SLOTS + s] = near * 8 + ((z - (g >> 1)) & 7)

    pltpu.make_async_copy(qh, qh, lq).wait()
    pl.semaphore_wait(barrier, 23)

    for off in Z_FAR:
        zz, device = z_peer(off)
        remote(qh.at[zz], qall.at[off], sa, ra.at[off], device).start()
    qall[0] = qh[z]

    for q in range(2):
        remote(quarter(q, 1 - core), w.at[1, q], sw, rw, sibling).start()

    for off in (0,) + Z_NEAR:
        block = qall.at[off]
        if off != 0:
            remote(qh.at[0], block, sa, ra.at[off], (me, tp)).wait_recv()
        for boff in B_FAR:
            slot = (boff[0] * 2 + boff[1]) * 8 + off
            remote(block, qall.at[slot], sb, rb, b_peer(boff)[1]).start()
    pltpu.make_async_copy(suf, suf, lsuf).wait()
    col = lax.broadcasted_iota(i32, (32, 512), 1)
    srow = lax.broadcasted_iota(i32, (32, 512), 0) & 15
    col_sample = col >> 5
    live_len = jnp.zeros((32, 512), i32)
    for s in range(SAMP):
        live_len = jnp.where(col_sample == s, len_s[s], live_len)
    live = (col_sample == srow) & ((col & 31) < live_len)
    lower = lax.broadcasted_iota(i32, (8, HD), 1) < 64
    for k in range(KVHEADS):
        query = qh[pl.ds(2 * k, 2)].reshape(32, HD)
        scores = (
            lax.dot_general(
                query, suf[0, k].reshape(512, HD), (((1,), (1,)), ((), ())),
                preferred_element_type=f32,
            )
            * SCORE_SCALE
        )
        top = jnp.max(jnp.where(live, scores, NEG), axis=1, keepdims=True)
        weights = jnp.where(live, jnp.exp(jnp.where(live, scores - top, 0.0)), 0.0)
        total = jnp.sum(weights, axis=1, keepdims=True)
        out = (
            jnp.dot(weights.astype(bf16), suf[1, k].reshape(512, HD), preferred_element_type=f32)
            / total
        )
        logs = jnp.broadcast_to(top + jnp.log(total), (32, HD))
        for h in range(2):
            at = h * SAMP
            sxs[2 * k + h, pl.ds(0, SAMP)] = out[at : at + SAMP]
            sxs[2 * k + h, pl.ds(SAMP, 8)] = jnp.where(
                lower, logs[at : at + 8], logs[at + 8 : at + 16]
            )
    for off in Z_FAR:
        zz, device = z_peer(off)
        remote(sxs.at[zz], sx.at[off], ssx, rsx, device).start()
    sx[0] = sxs[z]

    others = qall.at[pl.ds(8, 56)]
    remote(others, others, sb, rb, (me, tp)).wait_recv()

    for off in Z_FAR + (0,):
        for s in range(SLOTS):
            block = qall[slot_s[off * SLOTS + s]]
            if off == 0:
                qc[0, pl.ds(s * SAMP, SAMP)] = block
            else:
                csend[off, pl.ds(s * SAMP, SAMP)] = block
        if off != 0:
            remote(csend.at[off], qc.at[off], sc, rcs.at[off], z_peer(off)[1]).start()

    lane = lax.broadcasted_iota(i32, (1, 512), 1)
    lane_block = lane >> 4
    lane_row = lane & 15
    group_lane = jnp.zeros((1, 512), i32)
    prompt_lane = jnp.zeros((1, 512), i32)
    for c in range(32):
        group_lane = jnp.where(lane_block == c, pick_s[c], group_lane)
    for off in range(8):
        prompt_lane = jnp.where((lane >> 6) == off, own_p[off], prompt_lane)
    pick_b = (((group_lane >> 4) - x) & 3) * 2 + ((group_lane - yh) & 1)
    pick_z = ((group_lane >> 1) - z) & 7
    table = jnp.transpose(sam_v[...])
    member = jnp.zeros((PROMPTS, 512), f32)
    for s in range(SLOTS):
        member = member + jnp.where(table[:, s : s + 1] == group_lane, 1.0, 0.0)
    prompt_row = lax.broadcasted_iota(i32, (PROMPTS, 512), 0)
    count = jnp.sum(member, axis=0, keepdims=True)
    rank = jnp.sum(jnp.where(prompt_row < prompt_lane, member, 0.0), axis=0, keepdims=True)
    row = lane_row.astype(f32)
    rest = row - jnp.floor((row + 0.5) / count) * count
    owned = rest == rank
    place = jnp.where(owned, (pick_b * 8 + pick_z) * SAMP + lane_row, -1)
    place2 = jnp.where(owned, pick_b * SAMP + lane_row, -1)
    few = lax.broadcasted_iota(i32, (SAMP, 512), 0)

    def one_hot(first, wanted):
        return jnp.where(few + first * SAMP == wanted, 1.0, 0.0).astype(bf16)

    for n in range(8):
        for at, off in enumerate(Z_FAR[:3]):
            hot1[n, pl.ds(at * SAMP, SAMP)] = one_hot(n * 8 + off, place)
        hot1[n, pl.ds(48, SAMP)] = one_hot(n, place2)
        for at, off in enumerate(Z_FAR[3:] + (0,)):
            hot2[n, pl.ds(at * SAMP, SAMP)] = one_hot(n * 8 + off, place)
    tile_lane = lax.broadcasted_iota(i32, (SAMP, HD), 1)
    for c in range(32):
        of_z = ((pick_s[c] >> 1) - z) & 7
        keep = ((tile_lane >> 4) == of_z) & (((tile_lane & 15) >> 2) == c % SLOTS)
        lmask[pl.ds(c * SAMP, SAMP)] = jnp.where(keep, 1.0, 0.0).astype(bf16)

    pltpu.make_async_copy(kv, kv, lkv).wait()

    which_part = lax.broadcasted_iota(i32, (64, HD), 1) & 3
    which_slot = (tile_lane & 15) >> 2

    def attend(off):
        k = z_peer(-off)[0] // 2
        scores = (
            lax.dot_general(
                qc[off], kv[0, k], (((1,), (1,)), ((), ())), preferred_element_type=f32
            )
            * SCORE_SCALE
        )
        top = jnp.max(scores, axis=1, keepdims=True)
        weights = jnp.exp(scores - top)
        total = jnp.sum(weights, axis=1, keepdims=True)
        out = jnp.dot(weights.astype(bf16), kv[1, k], preferred_element_type=f32) / total
        log_total = top + jnp.log(total)
        wide = jnp.broadcast_to(log_total, (64, HD))
        high = wide.astype(bf16).astype(f32)
        middle = (wide - high).astype(bf16).astype(f32)
        low = wide - high - middle
        rest = jnp.where(which_part == 1, middle, jnp.where(which_part == 2, low, 0.0))
        parts = jnp.where(which_part == 0, high, rest)
        tile = parts[:SAMP]
        for s in range(1, SLOTS):
            tile = jnp.where(which_slot == s, parts[s * SAMP : (s + 1) * SAMP], tile)
        return out.astype(bf16), tile.astype(bf16)

    for group in ((4,), (3, 5), (2, 6), (1, 7), (0,)):
        for off in group:
            if off != 0:
                remote(csend.at[off], qc.at[off], sc, rcs.at[off], (me, tp)).wait_recv()
        results = [attend(off) for off in group]
        for off, (out, tile) in zip(group, results):
            result = rc if off == 0 else rsend
            result[off, pl.ds(0, 64)] = out
            result[off, pl.ds(64, SAMP)] = tile
            if off != 0:
                remote(
                    rsend.at[off], rc.at[off], sct, rct, z_peer(-off)[1]
                ).start()

    seven = rc.at[pl.ds(1, 7)]
    remote(seven, seven, sct, rct, (me, tp)).wait_recv()
    results = rc[:, pl.ds(0, 64)].reshape(512, HD)
    logs = jnp.concatenate(
        [rc[off, pl.ds(64, SAMP)] for off in range(8) for _ in range(SLOTS)], axis=0
    ) * lmask[...]
    both = jnp.concatenate([results, logs], axis=1)

    def from_b(boff):
        n = boff[0] * 2 + boff[1]
        first, second = (bt1, bt2) if n == 0 else (bsend1, bsend2)
        return n, first.at[n], second.at[n]

    for boff in B_FAR + ((0, 0),):
        n, first, _ = from_b(boff)
        picked = jnp.dot(hot1[n], both, preferred_element_type=f32).astype(bf16)
        first[pl.ds(0, 48)] = picked[:48, :HD]
        first[pl.ds(48, SAMP)] = picked[48:, HD:]
        if n != 0:
            remote(first, bt1.at[n], sbt.at[0], rbt.at[0], b_peer(boff)[1]).start()
    for boff in B_FAR + ((0, 0),):
        n, _, second = from_b(boff)
        second[...] = jnp.dot(hot2[n], results, preferred_element_type=f32).astype(bf16)
        if n != 0:
            remote(second, bt2.at[n], sbt.at[1], rbt.at[1], b_peer(boff)[1]).start()

    def merge(ref):
        merged = ref[0].astype(f32)
        for n in range(1, 8):
            merged = merged + ref[n].astype(f32)
        return merged

    def give(off, prefix_out):
        prefix_log = jnp.sum(
            jnp.where((tile_lane >> 4) == off, logs, 0.0), axis=1, keepdims=True
        )
        suffix = sx[(8 - off) % 8]
        suffix_log = jnp.concatenate([suffix[SAMP:, :1], suffix[SAMP:, 64:65]], axis=0)
        joint = jnp.maximum(prefix_log, suffix_log)
        share_p = jnp.exp(prefix_log - joint)
        share_s = jnp.exp(suffix_log - joint)
        attended = (share_p * prefix_out + share_s * suffix[:SAMP]) / (share_p + share_s)
        asend[off] = attended.astype(bf16)
        if off == 0:
            fin[0] = asend[0]
            remote(asend.at[0], fin.at[8], sat, rat, sibling).start()
        else:
            remote(asend.at[off], fin.at[off], sat, rat, z_peer(off)[1]).start()
            remote(asend.at[off], fin.at[8 + off], sat, rat, z_sibling(off)).start()

    seven = sx.at[pl.ds(1, 7)]
    remote(seven, seven, ssx, rsx, (me, tp)).wait_recv()
    seven = bt1.at[pl.ds(1, 7)]
    remote(seven, seven, sbt.at[0], rbt.at[0], (me, tp)).wait_recv()
    merged = merge(bt1)
    logs = merged[48:]
    for at, off in enumerate(Z_FAR[:3]):
        give(off, merged[at * SAMP : (at + 1) * SAMP])
    seven = bt2.at[pl.ds(1, 7)]
    remote(seven, seven, sbt.at[1], rbt.at[1], (me, tp)).wait_recv()
    merged = merge(bt2)
    for at, off in enumerate(Z_FAR[3:] + (0,)):
        give(off, merged[at * SAMP : (at + 1) * SAMP])
    pltpu.make_async_copy(w.at[0], w.at[0], lw).wait()
    remote(w.at[0], w.at[1], sw, rw, sibling).wait_recv()
    others = fin.at[pl.ds(0, 15)]
    remote(others, others, sat, rat, (me, tp)).wait_recv()

    attended = [
        jnp.concatenate([fin[side * 8 + (z - i) % 8] for i in range(HEADS)], axis=1)
        for side in range(2)
    ]

    def project(q, slot):
        parts = []
        for start, stop in ((0, 512), (512, COLS)):
            at = pl.ds(start, stop - start)
            part = sum(
                jnp.dot(attended[side], w[side, q, :, at], preferred_element_type=f32)
                for side in range(2)
            )
            psend[slot, :, at] = part.astype(bf16)
            remote(psend.at[slot, :, at], pr.at[slot, :, at], srs, rrs, across).start()
            parts.append(part)
        return jnp.concatenate(parts, axis=1)

    other_part = project(1 - chip, 0)
    own_part = project(chip, 1)
    for copy in small:
        copy.wait()
    remote(psend, pr, srs, rrs, across).wait_recv()
    projected = own_part + pr[0].astype(f32)
    twin = other_part + pr[1].astype(f32)
    squares = jnp.zeros((SAMP, HD), f32)
    for n in range(COLS // HD):
        for whole in (projected, twin):
            piece = whole[:, n * HD : (n + 1) * HD]
            squares = squares + piece * piece
    sqs[...] = squares
    remote(sqs, sqr, ssq, rsq, sibling).start()
    remote(sqs, sqr, ssq, rsq, sibling).wait_recv()
    squares = squares + sqr[...]
    scale = lax.rsqrt(jnp.sum(squares, axis=1, keepdims=True) / D + NORM_EPS)
    o_ref[...] = (res[...].astype(f32) + projected * scale * gain[...].reshape(1, COLS)).astype(bf16)

    for ref, count, send, recv in (
        (qall, 7, sa, ra.at[0]), (qall, 56, sb, rb), (csend, 7, sc, rcs.at[0]),
        (rc, 7, sct, rct), (bt1, 7, sbt.at[0], rbt.at[0]), (bt2, 7, sbt.at[1], rbt.at[1]),
        (sx, 7, ssx, rsx), (fin, 15, sat, rat),
    ):
        some = ref.at[pl.ds(0, count)]
        remote(some, some, send, recv, (me, tp)).wait_send()
    remote(w.at[0], w.at[1], sw, rw, sibling).wait_send()
    remote(psend, pr, srs, rrs, across).wait_send()
    remote(sqs, sqr, ssq, rsq, sibling).wait_send()


def shards(
    queries, prefix_kv, suffix_kv, suffix_len, prefill_group, sampler_groups,
    out_weight, norm_gain, residual,
):
    vmem = pltpu.VMEM
    dma = pltpu.SemaphoreType.DMA
    scratch = [
        vmem((HEADS, SAMP, HD), bf16),
        vmem((2, KVHEADS, PREFIX, HD), bf16),
        vmem((2, KVHEADS, SAMP, SUF, HD), bf16),
        vmem((2, 2, HEADS * HD, COLS), bf16),
        vmem((COLS,), f32),
        vmem((SAMP, COLS), bf16),
        pltpu.SMEM((SAMP,), i32),
        pltpu.SMEM((PROMPTS,), i32),
        pltpu.SMEM((SLOTS, PROMPTS), i32),
        vmem((SLOTS, PROMPTS), i32),
        pltpu.SMEM((8,), i32),
        pltpu.SMEM((32,), i32),
        pltpu.SMEM((32,), i32),
        vmem((64, SAMP, HD), bf16),
        vmem((8, 64, HD), bf16),
        vmem((8, 64, HD), bf16),
        vmem((8, 80, HD), bf16),
        vmem((8, 80, HD), bf16),
        vmem((8, 64, HD), bf16),
        vmem((8, 80, HD), bf16),
        vmem((8, 64, HD), bf16),
        vmem((8, 80, HD), bf16),
        vmem((8, SAMP, HD), bf16),
        vmem((16, SAMP, HD), bf16),
        vmem((8, 64, 512), bf16),
        vmem((8, 80, 512), bf16),
        vmem((512, HD), bf16),
        vmem((8, 24, HD), f32),
        vmem((8, 24, HD), f32),
        vmem((2, SAMP, COLS), bf16),
        vmem((2, SAMP, COLS), bf16),
        vmem((SAMP, HD), f32),
        vmem((SAMP, HD), f32),
        dma, dma, dma, dma, dma((2,)), dma((4,)),
        dma, dma((8,)),
        dma, dma,
        dma, dma((8,)),
        dma, dma,
        dma((2,)), dma((2,)),
        dma, dma,
        dma, dma,
        dma, dma,
        dma, dma,
        dma, dma,
    ]
    anywhere = pl.BlockSpec(memory_space=pl.ANY)
    return pl.pallas_call(
        kernel,
        out_shape=jax.ShapeDtypeStruct(residual.shape, bf16),
        in_specs=[anywhere] * 9,
        out_specs=pl.BlockSpec(memory_space=pltpu.VMEM),
        scratch_shapes=scratch,
        compiler_params=pltpu.CompilerParams(
            collective_id=0, has_side_effects=True, vmem_limit_bytes=48 * 1024 * 1024
        ),
        cost_estimate=pl.CostEstimate(
            flops=500_000_000, bytes_accessed=13_000_000, transcendentals=600_000
        ),
    )(
        *[
            pltpu.with_memory_space_constraint(operand, pltpu.HBM)
            for operand in (
                queries, prefix_kv, suffix_kv, suffix_len, prefill_group, sampler_groups.T,
                out_weight, norm_gain, residual,
            )
        ]
    )


def solution(mesh):
    in_specs = (
        P("grp", "tp"),
        P("grp", None, None, "tp"),
        P("grp", None, None, "tp"),
        P("grp"),
        P(),
        P(),
        P("tp", None),
        P("tp"),
        P("grp", "tp"),
    )
    return jax.shard_map(
        shards, mesh=mesh, in_specs=in_specs, out_specs=P("grp", "tp"), check_vma=False
    )
```

```python
import jax
import jax.numpy as jnp
from jax import lax
from jax.experimental import pallas as pl
from jax.experimental.pallas import tpu as pltpu
from jax.sharding import PartitionSpec as P

MESH = pl.DeviceIdType.MESH
D = 4608
HD = 128
SAMP = 16
SLOTS = 4
PREFIX = 1024
SUF = 32
HEADS = 8
KVHEADS = 4
COLS = 1152
PROMPTS = 64
SCORE_SCALE = 144.0 ** (-0.5)
NORM_EPS = 1e-06
NEG = -1e30

Z_FAR = (4, 3, 5, 2, 6, 1, 7)
Z_NEAR = (1, 7, 2, 6, 3, 5, 4)
B_FAR = ((2, 1), (1, 1), (3, 1), (2, 0), (0, 1), (1, 0), (3, 0))

f32 = jnp.float32
bf16 = jnp.bfloat16
i32 = jnp.int32


def kernel(
    q_hbm, kv_hbm, suf_hbm, len_hbm, pre_hbm, sam_hbm, w_hbm, gain_hbm, res_hbm,
    o_ref,
    qh, kv, suf, w, gain, res, len_s, pre_s, sam_s, sam_v,
    own_p, pick_s,
    qall, csend, qc, rsend, rc, bsend1, bsend2, bt1, bt2, asend, fin,
    hot1, hot2, lmask, sxs, sx, psend, pr, sqs, sqr,
    lq, lkv, lsuf, lw, lsmall, lint,
    sa, ra, sb, rb, sc, rcs, sct, rct, sbt, rbt, sat, rat, srs, rrs, ssq, rsq, sw, rw, ssx, rsx,
):
    me = lax.axis_index("grp")
    tp = lax.axis_index("tp")
    x = me // 16
    z = (me // 2) % 8
    yh = me % 2
    b = x * 2 + yh

    def grp_of(xx, zz, yy):
        return (xx * 8 + zz) * 2 + yy

    def z_peer(off):
        zz = (z + off) % 8
        return zz, (grp_of(x, zz, yh), tp)

    def b_peer(off):
        xx = (x + off[0]) % 4
        yy = (yh + off[1]) % 2
        return xx * 2 + yy, (grp_of(xx, z, yy), tp)

    chip, core = tp // 2, tp % 2
    sibling_tp = chip * 2 + (1 - core)
    sibling = (me, sibling_tp)
    across = (me, (1 - chip) * 2 + core)

    def z_sibling(off):
        return (grp_of(x, (z + off) % 8, yh), sibling_tp)

    def remote(src, dst, send, recv, device):
        return pltpu.make_async_remote_copy(
            src_ref=src, dst_ref=dst, send_sem=send, recv_sem=recv,
            device_id=device, device_id_type=MESH,
        )

    barrier = pltpu.get_barrier_semaphore()
    for off in Z_FAR:
        pl.semaphore_signal(barrier, inc=1, device_id=z_peer(off)[1], device_id_type=MESH)
    for off in B_FAR:
        pl.semaphore_signal(barrier, inc=1, device_id=b_peer(off)[1], device_id_type=MESH)
    for off in Z_FAR:
        pl.semaphore_signal(barrier, inc=1, device_id=z_sibling(off), device_id_type=MESH)
    for device in (across, sibling):
        pl.semaphore_signal(barrier, inc=1, device_id=device, device_id_type=MESH)

    ints = [
        pltpu.make_async_copy(pre_hbm, pre_s, lint.at[0]),
        pltpu.make_async_copy(sam_hbm, sam_s, lint.at[1]),
        pltpu.make_async_copy(sam_hbm, sam_v, lint.at[2]),
        pltpu.make_async_copy(len_hbm, len_s, lint.at[3]),
    ]
    for copy in ints:
        copy.start()
    for i in range(HEADS):
        pltpu.make_async_copy(q_hbm.at[:, pl.ds(i * HD, HD)], qh.at[i], lq).start()
    for part in range(2):
        for k in range(KVHEADS):
            pltpu.make_async_copy(
                kv_hbm.at[0, part, :, pl.ds(k * HD, HD)], kv.at[part, k], lkv
            ).start()
    for part in range(2):
        for k in range(KVHEADS):
            pltpu.make_async_copy(
                suf_hbm.at[:, part, :, pl.ds(k * HD, HD)], suf.at[part, k], lsuf
            ).start()
    small = [
        pltpu.make_async_copy(gain_hbm, gain, lsmall.at[0]),
        pltpu.make_async_copy(res_hbm, res, lsmall.at[1]),
    ]
    for copy in small:
        copy.start()

    def quarter(q, of_core):
        return w_hbm.at[:, pl.ds(pl.multiple_of((2 * q + of_core) * COLS, HD), COLS)]

    for q in range(2):
        pltpu.make_async_copy(quarter(q, core), w.at[q, 0], lw).start()

    for copy in ints:
        copy.wait()

    line = [z_peer(off)[1][0] for off in range(8)]

    def find(p, found):
        group = pre_s[p]
        return tuple(found[off] + jnp.where(group == line[off], p, 0) for off in range(8))

    found = lax.fori_loop(0, PROMPTS, find, (jnp.int32(0),) * 8)
    for off in range(8):
        own_p[off] = found[off]
        for s in range(SLOTS):
            pick_s[off * SLOTS + s] = sam_s[s, found[off] & 63]

    pltpu.make_async_copy(qh, qh, lq).wait()
    pl.semaphore_wait(barrier, 23)

    for off in Z_FAR:
        zz, device = z_peer(off)
        remote(qh.at[zz], qall.at[off], sa, ra.at[off], device).start()
    qall[0] = qh[z]

    for q in range(2):
        remote(quarter(q, 1 - core), w.at[q, 1], sw, rw, sibling).start()

    for off in (0,) + Z_NEAR:
        block = qall.at[off]
        if off != 0:
            remote(qh.at[0], block, sa, ra.at[off], (me, tp)).wait_recv()
        for boff in B_FAR:
            slot = (boff[0] * 2 + boff[1]) * 8 + off
            remote(block, qall.at[slot], sb, rb, b_peer(boff)[1]).start()
    pltpu.make_async_copy(suf, suf, lsuf).wait()
    col = lax.broadcasted_iota(i32, (32, 512), 1)
    srow = lax.broadcasted_iota(i32, (32, 512), 0) & 15
    col_sample = col >> 5
    live_len = jnp.zeros((32, 512), i32)
    for s in range(SAMP):
        live_len = jnp.where(col_sample == s, len_s[s], live_len)
    live = (col_sample == srow) & ((col & 31) < live_len)
    lower = lax.broadcasted_iota(i32, (8, HD), 1) < 64
    for k in range(KVHEADS):
        query = qh[pl.ds(2 * k, 2)].reshape(32, HD)
        scores = (
            lax.dot_general(
                query, suf[0, k].reshape(512, HD), (((1,), (1,)), ((), ())),
                preferred_element_type=f32,
            )
            * SCORE_SCALE
        )
        top = jnp.max(jnp.where(live, scores, NEG), axis=1, keepdims=True)
        weights = jnp.where(live, jnp.exp(jnp.where(live, scores - top, 0.0)), 0.0)
        total = jnp.sum(weights, axis=1, keepdims=True)
        out = (
            jnp.dot(weights.astype(bf16), suf[1, k].reshape(512, HD), preferred_element_type=f32)
            / total
        )
        logs = jnp.broadcast_to(top + jnp.log(total), (32, HD))
        for h in range(2):
            at = h * SAMP
            sxs[2 * k + h, pl.ds(0, SAMP)] = out[at : at + SAMP]
            sxs[2 * k + h, pl.ds(SAMP, 8)] = jnp.where(
                lower, logs[at : at + 8], logs[at + 8 : at + 16]
            )
    for off in Z_FAR:
        zz, device = z_peer(off)
        remote(sxs.at[zz], sx.at[off], ssx, rsx, device).start()
    sx[0] = sxs[z]

    others = qall.at[pl.ds(8, 56)]
    remote(others, others, sb, rb, (me, tp)).wait_recv()

    for off in Z_FAR + (0,):
        for s in range(SLOTS):
            g = pick_s[off * SLOTS + s]
            slot = (((x - (g >> 4)) & 3) * 2 + ((yh - g) & 1)) * 8 + ((z - (g >> 1)) & 7)
            block = qall[slot]
            if off == 0:
                qc[0, pl.ds(s * SAMP, SAMP)] = block
            else:
                csend[off, pl.ds(s * SAMP, SAMP)] = block
        if off != 0:
            remote(csend.at[off], qc.at[off], sc, rcs.at[off], z_peer(off)[1]).start()

    lane = lax.broadcasted_iota(i32, (1, 512), 1)
    lane_block = lane >> 4
    lane_row = lane & 15
    group_lane = jnp.zeros((1, 512), i32)
    prompt_lane = jnp.zeros((1, 512), i32)
    for c in range(32):
        group_lane = jnp.where(lane_block == c, pick_s[c], group_lane)
    for off in range(8):
        prompt_lane = jnp.where((lane >> 6) == off, own_p[off], prompt_lane)
    pick_b = (((group_lane >> 4) - x) & 3) * 2 + ((group_lane - yh) & 1)
    pick_z = ((group_lane >> 1) - z) & 7
    table = jnp.transpose(sam_v[...])
    member = jnp.zeros((PROMPTS, 512), f32)
    for s in range(SLOTS):
        member = member + jnp.where(table[:, s : s + 1] == group_lane, 1.0, 0.0)
    prompt_row = lax.broadcasted_iota(i32, (PROMPTS, 512), 0)
    count = jnp.sum(member, axis=0, keepdims=True)
    rank = jnp.sum(jnp.where(prompt_row < prompt_lane, member, 0.0), axis=0, keepdims=True)
    row = lane_row.astype(f32)
    rest = row - jnp.floor((row + 0.5) / count) * count
    owned = rest == rank
    place = jnp.where(owned, (pick_b * 8 + pick_z) * SAMP + lane_row, -1)
    place2 = jnp.where(owned, pick_b * SAMP + lane_row, -1)
    few = lax.broadcasted_iota(i32, (SAMP, 512), 0)

    def one_hot(first, wanted):
        return jnp.where(few + first * SAMP == wanted, 1.0, 0.0).astype(bf16)

    for n in range(8):
        for at, off in enumerate(Z_FAR[:3]):
            hot1[n, pl.ds(at * SAMP, SAMP)] = one_hot(n * 8 + off, place)
        hot1[n, pl.ds(48, SAMP)] = one_hot(n, place2)
        for at, off in enumerate(Z_FAR[3:] + (0,)):
            hot2[n, pl.ds(at * SAMP, SAMP)] = one_hot(n * 8 + off, place)
    tile_lane = lax.broadcasted_iota(i32, (SAMP, HD), 1)
    for c in range(32):
        of_z = ((pick_s[c] >> 1) - z) & 7
        keep = ((tile_lane >> 3) == of_z) & (((tile_lane & 7) >> 1) == c % SLOTS)
        lmask[pl.ds(c * SAMP, SAMP)] = jnp.where(keep, 1.0, 0.0).astype(bf16)

    pltpu.make_async_copy(kv, kv, lkv).wait()

    def attend(off):
        k = z_peer(-off)[0] // 2
        scores = (
            lax.dot_general(
                qc[off], kv[0, k], (((1,), (1,)), ((), ())), preferred_element_type=f32
            )
            * SCORE_SCALE
        )
        top = jnp.max(scores, axis=1, keepdims=True)
        weights = jnp.exp(scores - top)
        total = jnp.sum(weights, axis=1, keepdims=True)
        out = jnp.dot(weights.astype(bf16), kv[1, k], preferred_element_type=f32) / total
        log_total = top + jnp.log(total)
        high = log_total.astype(bf16).astype(f32)
        low = log_total - high
        tile = jnp.zeros((SAMP, HD), f32)
        for s in range(SLOTS):
            at = s * SAMP
            tile = jnp.where((tile_lane & 7) == 2 * s, high[at : at + SAMP], tile)
            tile = jnp.where((tile_lane & 7) == 2 * s + 1, low[at : at + SAMP], tile)
        return out.astype(bf16), tile.astype(bf16)

    for group in ((4,), (3, 5), (2, 6), (1, 7), (0,)):
        for off in group:
            if off != 0:
                remote(csend.at[off], qc.at[off], sc, rcs.at[off], (me, tp)).wait_recv()
        results = [attend(off) for off in group]
        for off, (out, tile) in zip(group, results):
            result = rc if off == 0 else rsend
            result[off, pl.ds(0, 64)] = out
            result[off, pl.ds(64, SAMP)] = tile
            if off != 0:
                remote(
                    rsend.at[off], rc.at[off], sct, rct, z_peer(-off)[1]
                ).start()

    seven = rc.at[pl.ds(1, 7)]
    remote(seven, seven, sct, rct, (me, tp)).wait_recv()
    results = rc[:, pl.ds(0, 64)].reshape(512, HD)
    logs = jnp.concatenate(
        [rc[off, pl.ds(64, SAMP)] for off in range(8) for _ in range(SLOTS)], axis=0
    ) * lmask[...]
    both = jnp.concatenate([results, logs], axis=1)

    def from_b(boff):
        n = boff[0] * 2 + boff[1]
        first, second = (bt1, bt2) if n == 0 else (bsend1, bsend2)
        return n, first.at[n], second.at[n]

    for boff in B_FAR + ((0, 0),):
        n, first, _ = from_b(boff)
        picked = jnp.dot(hot1[n], both, preferred_element_type=f32).astype(bf16)
        first[pl.ds(0, 48)] = picked[:48, :HD]
        first[pl.ds(48, SAMP)] = picked[48:, HD:]
        if n != 0:
            remote(first, bt1.at[n], sbt.at[0], rbt.at[0], b_peer(boff)[1]).start()
    for boff in B_FAR + ((0, 0),):
        n, _, second = from_b(boff)
        second[...] = jnp.dot(hot2[n], results, preferred_element_type=f32).astype(bf16)
        if n != 0:
            remote(second, bt2.at[n], sbt.at[1], rbt.at[1], b_peer(boff)[1]).start()

    def merge(ref):
        merged = ref[0].astype(f32)
        for n in range(1, 8):
            merged = merged + ref[n].astype(f32)
        return merged

    def give(off, prefix_out):
        prefix_log = jnp.sum(
            jnp.where((tile_lane >> 3) == off, logs, 0.0), axis=1, keepdims=True
        )
        suffix = sx[(8 - off) % 8]
        suffix_log = jnp.concatenate([suffix[SAMP:, :1], suffix[SAMP:, 64:65]], axis=0)
        joint = jnp.maximum(prefix_log, suffix_log)
        share_p = jnp.exp(prefix_log - joint)
        share_s = jnp.exp(suffix_log - joint)
        attended = (share_p * prefix_out + share_s * suffix[:SAMP]) / (share_p + share_s)
        asend[off] = attended.astype(bf16)
        if off == 0:
            fin[0] = asend[0]
            remote(asend.at[0], fin.at[8], sat, rat, sibling).start()
        else:
            remote(asend.at[off], fin.at[off], sat, rat, z_peer(off)[1]).start()
            remote(asend.at[off], fin.at[8 + off], sat, rat, z_sibling(off)).start()

    seven = sx.at[pl.ds(1, 7)]
    remote(seven, seven, ssx, rsx, (me, tp)).wait_recv()
    seven = bt1.at[pl.ds(1, 7)]
    remote(seven, seven, sbt.at[0], rbt.at[0], (me, tp)).wait_recv()
    merged = merge(bt1)
    logs = merged[48:]
    for at, off in enumerate(Z_FAR[:3]):
        give(off, merged[at * SAMP : (at + 1) * SAMP])
    seven = bt2.at[pl.ds(1, 7)]
    remote(seven, seven, sbt.at[1], rbt.at[1], (me, tp)).wait_recv()
    merged = merge(bt2)
    for at, off in enumerate(Z_FAR[3:] + (0,)):
        give(off, merged[at * SAMP : (at + 1) * SAMP])
    pltpu.make_async_copy(w.at[0], w.at[0], lw).wait()
    remote(w.at[0], w.at[1], sw, rw, sibling).wait_recv()
    others = fin.at[pl.ds(0, 15)]
    remote(others, others, sat, rat, (me, tp)).wait_recv()

    attended = jnp.concatenate(
        [fin[side * 8 + (z - i) % 8] for side in range(2) for i in range(HEADS)], axis=1
    )

    def project(q, slot):
        parts = []
        for start, stop in ((0, 512), (512, COLS)):
            at = pl.ds(start, stop - start)
            part = jnp.dot(
                attended, w[q, :, :, at].reshape(2 * HEADS * HD, stop - start),
                preferred_element_type=f32,
            )
            psend[slot, :, at] = part.astype(bf16)
            remote(
                psend.at[slot, :, at], pr.at[slot, :, at], srs, rrs.at[slot], across
            ).start()
            parts.append(part)
        return jnp.concatenate(parts, axis=1)

    other_part = project(1 - chip, 0)
    own_part = project(chip, 1)
    for copy in small:
        copy.wait()
    def finish(part, slot, squares):
        remote(psend.at[slot], pr.at[slot], srs, rrs.at[slot], across).wait_recv()
        whole = part + pr[slot].astype(f32)
        for n in range(COLS // HD):
            piece = whole[:, n * HD : (n + 1) * HD]
            squares = squares + piece * piece
        return whole, squares

    projected, squares = finish(own_part, 0, jnp.zeros((SAMP, HD), f32))
    _, squares = finish(other_part, 1, squares)
    sqs[...] = squares
    remote(sqs, sqr, ssq, rsq, sibling).start()
    remote(sqs, sqr, ssq, rsq, sibling).wait_recv()
    squares = squares + sqr[...]
    scale = lax.rsqrt(jnp.sum(squares, axis=1, keepdims=True) / D + NORM_EPS)
    o_ref[...] = (res[...].astype(f32) + projected * scale * gain[...].reshape(1, COLS)).astype(bf16)

    for ref, count, send, recv in (
        (qall, 7, sa, ra.at[0]), (qall, 56, sb, rb), (csend, 7, sc, rcs.at[0]),
        (rc, 7, sct, rct), (bt1, 7, sbt.at[0], rbt.at[0]), (bt2, 7, sbt.at[1], rbt.at[1]),
        (sx, 7, ssx, rsx), (fin, 15, sat, rat),
    ):
        some = ref.at[pl.ds(0, count)]
        remote(some, some, send, recv, (me, tp)).wait_send()
    remote(w.at[0], w.at[1], sw, rw, sibling).wait_send()
    remote(psend, pr, srs, rrs.at[0], across).wait_send()
    remote(sqs, sqr, ssq, rsq, sibling).wait_send()


def shards(
    queries, prefix_kv, suffix_kv, suffix_len, prefill_group, sampler_groups,
    out_weight, norm_gain, residual,
):
    vmem = pltpu.VMEM
    dma = pltpu.SemaphoreType.DMA
    scratch = [
        vmem((HEADS, SAMP, HD), bf16),
        vmem((2, KVHEADS, PREFIX, HD), bf16),
        vmem((2, KVHEADS, SAMP, SUF, HD), bf16),
        vmem((2, 2, HEADS * HD, COLS), bf16),
        vmem((COLS,), f32),
        vmem((SAMP, COLS), bf16),
        pltpu.SMEM((SAMP,), i32),
        pltpu.SMEM((PROMPTS,), i32),
        pltpu.SMEM((SLOTS, PROMPTS), i32),
        vmem((SLOTS, PROMPTS), i32),
        pltpu.SMEM((8,), i32),
        pltpu.SMEM((32,), i32),
        vmem((64, SAMP, HD), bf16),
        vmem((8, 64, HD), bf16),
        vmem((8, 64, HD), bf16),
        vmem((8, 80, HD), bf16),
        vmem((8, 80, HD), bf16),
        vmem((8, 64, HD), bf16),
        vmem((8, 80, HD), bf16),
        vmem((8, 64, HD), bf16),
        vmem((8, 80, HD), bf16),
        vmem((8, SAMP, HD), bf16),
        vmem((16, SAMP, HD), bf16),
        vmem((8, 64, 512), bf16),
        vmem((8, 80, 512), bf16),
        vmem((512, HD), bf16),
        vmem((8, 24, HD), f32),
        vmem((8, 24, HD), f32),
        vmem((2, SAMP, COLS), bf16),
        vmem((2, SAMP, COLS), bf16),
        vmem((SAMP, HD), f32),
        vmem((SAMP, HD), f32),
        dma, dma, dma, dma, dma((2,)), dma((4,)),
        dma, dma((8,)),
        dma, dma,
        dma, dma((8,)),
        dma, dma,
        dma((2,)), dma((2,)),
        dma, dma,
        dma, dma((2,)),
        dma, dma,
        dma, dma,
        dma, dma,
    ]
    anywhere = pl.BlockSpec(memory_space=pl.ANY)
    return pl.pallas_call(
        kernel,
        out_shape=jax.ShapeDtypeStruct(residual.shape, bf16),
        in_specs=[anywhere] * 9,
        out_specs=pl.BlockSpec(memory_space=pltpu.VMEM),
        scratch_shapes=scratch,
        compiler_params=pltpu.CompilerParams(
            collective_id=0, has_side_effects=True, vmem_limit_bytes=48 * 1024 * 1024
        ),
        cost_estimate=pl.CostEstimate(
            flops=500_000_000, bytes_accessed=13_000_000, transcendentals=600_000
        ),
    )(
        *[
            pltpu.with_memory_space_constraint(operand, pltpu.HBM)
            for operand in (
                queries, prefix_kv, suffix_kv, suffix_len, prefill_group, sampler_groups.T,
                out_weight, norm_gain, residual,
            )
        ]
    )


def solution(mesh):
    in_specs = (
        P("grp", "tp"),
        P("grp", None, None, "tp"),
        P("grp", None, None, "tp"),
        P("grp"),
        P(),
        P(),
        P("tp", None),
        P("tp"),
        P("grp", "tp"),
    )
    return jax.shard_map(
        shards, mesh=mesh, in_specs=in_specs, out_specs=P("grp", "tp"), check_vma=False
    )
```
